32 devices in a mesh: groups: 2 (over y), wide: 16 (over z, x, core).
Axes of the slice: x: 2, y: 2, z: 4, core: 2. Of those that a mesh axis runs over, the one named last changes fastest.
Arguments:
- density: bfloat16 [4096, 2048], P(('groups', 'wide')), parts along dimension 0, may hold values from -0.0234375 to 0.0234375
- ao_values: bfloat16 [2048, 2, 32, 128], P(('groups', 'wide')), parts along dimension 0, may hold values from -6 to 6
- block_lists: int32 [2048, 2], P(('groups', 'wide')), parts along dimension 0, may hold values from 0 to 15, all different within a row; in each aligned block of 64 rows (0 to 63, 64 to 127, ...) at most 8 rows name the same one
- counts: int32 [2048], P(('groups', 'wide')), parts along dimension 0, may hold values from 1 to 2
- other_features: float32 [2048, 10, 32], P(('groups', 'wide')), parts along dimension 0, may hold values from -6 to 6
- quad_weights: float32 [2048, 32], P(('groups', 'wide')), parts along dimension 0, may hold values from 0.02 to 0.2
- w_in: float32 [11, 256], replicated, may hold values from -1.75 to 1.75
- biases: float32 [4, 256], replicated, may hold values from -2.5 to 2.5
- w_layers: bfloat16 [3, 256, 256], replicated, may hold values from -0.375 to 0.375
- w_out: float32 [256], replicated, may hold values from -0.375 to 0.375
Outputs:
- potential: bfloat16 [4096, 2048], P(('groups', 'wide')), parts along dimension 0
- weight_grads: float32 [6, 256, 256], P('groups'), parts along dimension 0
- input_grads: float32 [22, 256], P('groups'), parts along dimension 0
- bias_grads: float32 [8, 256], P('groups'), parts along dimension 0
- output_grads: float32 [512], P('groups'), parts along dimension 0
The draws below stay inside these ranges and needn't reach their ends.
There are 2 independent parts, one for each index of `groups`. The reference program is written for one: setup_inputs(seed, part) draws one part's arguments, and reference() takes and returns one part's arrays. A program takes and returns all parts, laid end to end along the dimension named above; an argument that names none is the same for every part. Nothing has to cross between parts.
Inputs may be any that keep to these rules, and one draw needn't show every extreme that they name: `block_lists`: the 2 entries of a batch are different blocks; among the 64 batches of one index of wide no block is named by more than 8 of them.
All inputs are finite; a program needn't handle non-finite values.
Results may differ from the reference program's by a relative error of at most 0.0035.
Values may be sent and summed in bfloat16 or wider, within the bound.
A program may use at most 128 MiB of HBM per device.

```python
import math
import jax
import jax.numpy as jnp
import numpy as np
from jax import lax

HID = 256
FEAT = 11
LAYERS = 3
BW = 128
PTS = 32
KMAX = 2
BATCH_DEV = 64
NBLK = 16
NBF = 2048
FO = 10
BATCHES = 1024
CAP = 8
N_WIDE = 16


def plant(drawn, stream_key, least, largest):
    place = [jax.random.randint(jax.random.fold_in(stream_key, axis), (), 0, length) for axis, length in enumerate(drawn.shape)]
    longest = drawn.shape.index(max(drawn.shape))
    neighbour = place[:longest] + [(place[longest] + 1) % drawn.shape[longest]] + place[longest + 1:]
    return drawn.at[tuple(place)].set(least).at[tuple(neighbour)].set(largest)


def levels(key, shape, pieces, smallest, top_value):
    level = 1.0
    for dim, shards_of in pieces:
        steps = jax.random.uniform(jax.random.fold_in(jax.random.fold_in(key, 6), dim), (shards_of,), jnp.float32, smallest / len(pieces), top_value / len(pieces))
        level = level * jnp.repeat(jnp.exp(steps), shape[dim] // shards_of).reshape((-1,) + (1,) * (len(shape) - 1 - dim))
    return level


def shared_out(key, own, number, rows, count, top, bound, lean):
    ranking = jax.random.permutation(key, count)
    packed, ordinary = load_shares(count, rows * top, bound, lean, True), load_shares(count, rows * top, bound, lean, False)
    places = jnp.arange(count)

    def named(tallies, turn):
        used = int((tallies > 0).sum())
        fixed = max(1, used // 4)
        shifted = fixed + (places - fixed + turn * (used - fixed)) % max(1, count - fixed)
        return jnp.zeros((count,), jnp.int32).at[ranking[jnp.where(places < fixed, places, shifted)]].set(jnp.asarray(tallies, jnp.int32))

    tallies = jnp.where(number % 4 == 0, named(packed, number // 4), named(ordinary, number - number // 4 - 1))
    mixed = jax.random.permutation(jax.random.fold_in(own, 3), count)
    source_of, taker = mixed[0:count // 2 * 2:2], mixed[1:count // 2 * 2:2]
    margin = jnp.minimum(tallies[source_of] - 1, bound - tallies[taker]) // 2
    margin = jnp.where((source_of == ranking[0]) | (taker == ranking[0]) | (tallies[taker] == 0), 0, jnp.maximum(margin, 0))
    shifted = jax.random.randint(jax.random.fold_in(own, 4), (count // 2,), 0, 1 << 20) % (margin + 1)
    tallies = tallies.at[source_of].add(-shifted).at[taker].add(shifted)
    labels = jnp.searchsorted(jnp.cumsum(tallies), jnp.arange(rows * top), side="right").astype(jnp.int32)
    listing = labels.reshape(top, rows).T
    listing = listing[jax.random.permutation(jax.random.fold_in(own, 1), rows)]
    turn = jax.random.randint(jax.random.fold_in(own, 2), (rows, 1), 0, top)
    return jnp.take_along_axis(listing, (jnp.arange(top)[None, :] + turn) % top, axis=1)


def load_shares(number_of, total, reach, slope, full):
    portions = [(1 << 20) // math.isqrt(grade ** slope) + 1 for grade in range(1, number_of + 1)]
    largest = reach if full else min(reach, max(-(-total // number_of), total * portions[0] // sum(portions)))
    least = 1 if total - largest >= number_of - 1 else 0
    holding, spare = [largest] + [least] * (number_of - 1), total - largest - least * (number_of - 1)
    while spare > 0:
        free = [i for i in range(1, number_of) if holding[i] < largest] or [i for i in range(1, number_of) if holding[i] < reach]
        mass, remaining = sum([portions[i] for i in free]), spare
        for i in free:
            addition = min(reach - holding[i], max(1, remaining * portions[i] // mass), spare)
            holding[i] = holding[i] + addition
            spare = spare - addition
    return np.array(holding)


def normal_values(stream_key, dims, deviation, most, cuts=(), kind=jnp.bfloat16):
    level = levels(stream_key, dims, cuts, -0.22, 0.18) if cuts else 1.0
    values = jax.random.normal(stream_key, dims, jnp.float32) * deviation * level
    return jnp.minimum(jnp.maximum(values, -most), most).astype(kind)


def setup_inputs(seed: int = 0, part: int = 0) -> dict:
    seeds = jax.random.split(jax.random.key(seed), 11)
    part_keys = jax.random.split(jax.random.fold_in(seeds[10], part), 11)
    density = normal_values(part_keys[0], (NBF, NBF), (1.0 / (KMAX * BW)), 0.0234375, ((0, 16),))
    ao_values = normal_values(part_keys[1], (BATCHES, KMAX, PTS, BW), 1.0, 6.0, ((0, 16),))
    block_lists_keys = jax.random.split(jax.random.fold_in(part_keys[2], 1), BATCHES // BATCH_DEV)
    block_lists_turns = jax.random.permutation(jax.random.fold_in(part_keys[2], 3), BATCHES // BATCH_DEV)
    block_lists = jax.vmap(lambda own, number: shared_out(jax.random.fold_in(part_keys[2], 2), own, number, BATCH_DEV, NBLK, KMAX, CAP, 2))(block_lists_keys, block_lists_turns).reshape((BATCHES, KMAX))
    counts = plant(jax.random.randint(part_keys[3], (BATCHES,), 1, KMAX + 1), jax.random.fold_in(part_keys[3], 1), 1, KMAX).astype(jnp.int32)
    other_features = normal_values(part_keys[4], (BATCHES, FO, PTS), 1.0, 6.0, ((0, 16),), jnp.float32)
    quad_weights = jnp.clip(jnp.exp(math.log(0.2) - 2.3025851 * jax.random.uniform(part_keys[5], (BATCHES, PTS), jnp.float32) ** levels(part_keys[5], (BATCHES, PTS), ((0, 16),), -0.2, 0.2)), 0.02, 0.2)
    w_in = normal_values(seeds[6], (FEAT, HID), FEAT ** -0.5, 1.75, (), jnp.float32)
    biases = normal_values(seeds[7], (LAYERS + 1, HID), 0.5, 2.5, (), jnp.float32)
    w_layers = normal_values(seeds[8], (LAYERS, HID, HID), HID ** -0.5, 0.375)
    w_out = normal_values(seeds[9], (HID,), HID ** -0.5, 0.375, (), jnp.float32)
    return {"density": density, "ao_values": ao_values, "block_lists": block_lists, "counts": counts, "other_features": other_features, "quad_weights": quad_weights, "w_in": w_in, "biases": biases, "w_layers": w_layers, "w_out": w_out}


highest = lax.Precision.HIGHEST


def masked_batch(ao_batch, count_now):
    live_mask = jnp.arange(KMAX) < count_now
    return jnp.where(live_mask[:, None, None], ao_batch, jnp.zeros((), ao_batch.dtype))


def energy_grads(density_pts, other, weights_q, w_in, biases, w_layers, w_out):
    batch_count, point_count = density_pts.shape
    row_count = batch_count * point_count
    hidden_width = w_out.shape[0]
    layer_count = w_layers.shape[0]
    features = jnp.concatenate([density_pts[:, None, :], other], axis=1)
    pre_act = jnp.einsum("bfp,fh->bph", features, w_in, precision=highest) + biases[0]
    activations = [jnp.tanh(pre_act).reshape(row_count, hidden_width).astype(jnp.bfloat16)]
    for layer_idx in range(layer_count):
        inner_sum = jnp.dot(activations[-1], w_layers[layer_idx], preferred_element_type=jnp.float32) + biases[layer_idx + 1]
        activations.append(jnp.tanh(inner_sum).astype(jnp.bfloat16))
    top_act = activations[-1].astype(jnp.float32)
    out_score = jnp.dot(top_act, w_out, precision=highest)
    enhance = 2.0 * jax.nn.sigmoid(out_score)
    rho_flat = density_pts.reshape(row_count)
    weight_flat = weights_q.reshape(row_count)
    grad_score = weight_flat * rho_flat * enhance * (1.0 - 0.5 * enhance)
    out_grad = jnp.dot(grad_score, top_act, precision=highest)
    grad_act = grad_score[:, None] * w_out[None, :]
    layer_grads = [None] * layer_count
    bias_list = [None] * (layer_count + 1)
    for layer_idx in reversed(range(layer_count)):
        act_after = activations[layer_idx + 1].astype(jnp.float32)
        grad_pre = grad_act * (1.0 - act_after * act_after)
        grad_round = grad_pre.astype(jnp.bfloat16)
        layer_grads[layer_idx] = jnp.dot(activations[layer_idx].T, grad_round, preferred_element_type=jnp.float32)
        bias_list[layer_idx + 1] = jnp.sum(grad_pre, axis=0)
        grad_act = jnp.dot(grad_round, w_layers[layer_idx].T, preferred_element_type=jnp.float32)
    act_first = activations[0].astype(jnp.float32)
    grad_first = grad_act * (1.0 - act_first * act_first)
    bias_list[0] = jnp.sum(grad_first, axis=0)
    feature_rows = features.transpose(0, 2, 1).reshape(row_count, features.shape[1])
    input_term = jnp.dot(feature_rows.T, grad_first, precision=highest)
    grad_rho = jnp.dot(grad_first, w_in[0], precision=highest)
    potential_weight = (weight_flat * enhance + grad_rho).reshape(batch_count, point_count)
    return potential_weight, (jnp.stack(layer_grads), input_term, jnp.stack(bias_list), out_grad)


def reference(density, ao_values, block_lists, counts, other_features, quad_weights, w_in, biases, w_layers, w_out):
    blocks4 = density.reshape(NBLK, BW, NBLK, BW)

    def one_batch(items):
        phi_live = masked_batch(items[0], items[2])
        block_row = items[1]
        chosen = blocks4[block_row[:, None], :, block_row[None, :], :]
        phi_wide = phi_live.astype(jnp.float32)
        product = jnp.einsum("apm,acmq->acpq", phi_wide, chosen.astype(jnp.float32), precision=highest)
        return jnp.sum(product * phi_wide[None], axis=(0, 1, 3))

    density_pts = lax.map(one_batch, (ao_values, block_lists, counts))

    def grouped(array):
        return array.reshape((N_WIDE, BATCH_DEV) + array.shape[1:])

    def group_step(carry, items):
        weight_now, grads = energy_grads(items[0], items[1], items[2], w_in, biases, w_layers, w_out)
        return jax.tree.map(jnp.add, carry, grads), weight_now

    start = (jnp.zeros((LAYERS, HID, HID), jnp.float32), jnp.zeros((FEAT, HID), jnp.float32),
             jnp.zeros((LAYERS + 1, HID), jnp.float32), jnp.zeros((HID,), jnp.float32))
    sums, pot_weights = lax.scan(group_step, start, (grouped(density_pts), grouped(other_features), grouped(quad_weights)))
    pot_weights = pot_weights.reshape(BATCHES, PTS)

    def add_batch(accum, items):
        phi_live = masked_batch(items[0], items[2])
        block_row = items[1]
        weighted = (phi_live.astype(jnp.float32) * items[3][None, :, None]).astype(jnp.bfloat16)
        contrib = jnp.einsum("apm,cpq->acmq", weighted.astype(jnp.float32), phi_live.astype(jnp.float32), precision=highest)
        accum = accum.at[block_row[:, None], :, block_row[None, :], :].add(contrib)
        return accum, None

    accum, unused = lax.scan(add_batch, jnp.zeros((NBLK, BW, NBLK, BW), jnp.float32), (ao_values, block_lists, counts, pot_weights))
    potential = accum.reshape(NBF, NBF).astype(jnp.bfloat16)
    return potential, sums[0], sums[1], sums[2], sums[3]
```

```python
import functools

import jax
import jax.numpy as jnp
from jax import lax
from jax.experimental import pallas as pl
from jax.experimental.pallas import tpu as pltpu
from jax.sharding import PartitionSpec as P

highest = lax.Precision.HIGHEST
F32 = jnp.float32
BF16 = jnp.bfloat16
CHUNK = 512
VMEM = pl.BlockSpec(memory_space=pltpu.VMEM)
SMEM = pl.BlockSpec(memory_space=pltpu.SMEM)
PARAMS = pltpu.CompilerParams(vmem_limit_bytes=56 * 1024 * 1024)


def up8(x):
    return (x + 7) // 8 * 8


def eye_mask(points):
    return lax.broadcasted_iota(jnp.int32, (points, 128), 0) == lax.broadcasted_iota(
        jnp.int32, (points, 128), 1
    )


def col_dot(a, b):
    return lax.dot_general(a, b, (((0,), (0,)), ((), ())), preferred_element_type=F32)


def rho_kernel(cap, pid_ref, ao_ref, den_ref, out_ref):
    sources = ao_ref.shape[0]
    points, width = ao_ref.shape[3:]
    me = lax.axis_index("wide")
    own = den_ref[:, pl.ds(pl.multiple_of(me * width, width), width)]
    eye = eye_mask(points)

    def body(i, carry):
        rows = []
        for r in range(cap):
            c = pid_ref[i, r]
            other = den_ref[:, pl.ds(pl.multiple_of(c * width, width), width)]
            x = ao_ref[i, r, 0]
            y = ao_ref[i, r, 1]
            q = jnp.dot(x, own, preferred_element_type=F32) * x.astype(F32)
            q = q + jnp.dot(x, other, preferred_element_type=F32) * y.astype(F32)
            col = jnp.sum(q, axis=1, keepdims=True)
            rows.append(jnp.sum(jnp.where(eye, col, 0.0), axis=0, keepdims=True))
        pad = out_ref.shape[1] - cap
        if pad:
            rows.append(jnp.zeros((pad, 128), F32))
        out_ref[i] = jnp.concatenate(rows, axis=0)
        return carry

    lax.fori_loop(0, sources, body, 0)


def mlp_kernel(
    slot_ref, src_ref, ret_ref, pre_ref, feat_ref, quad_ref, win_ref, bias_ref, wl_ref, wout_ref,
    sendw_ref, grads_ref, rho_scr, quad_scr, pw_scr,
):
    batches, points = quad_ref.shape
    hidden = wout_ref.shape[1]
    layers = wl_ref.shape[0]
    slots = ret_ref.shape[0]
    eye = eye_mask(points)
    slot_no = lax.broadcasted_iota(jnp.int32, (batches, slots), 1)
    pick = (slot_no == slot_ref[:, 0:1]) | (slot_no == slot_ref[:, 1:2])
    rho = jnp.dot(pick.astype(F32), ret_ref[...], precision=highest, preferred_element_type=F32)
    rho_scr[...] = rho
    quad_scr[...] = jnp.zeros_like(quad_scr)
    quad_scr[:, 0:points] = quad_ref[...]
    grads_ref[...] = jnp.zeros_like(grads_ref)
    per = CHUNK // points
    small = layers * hidden
    features = feat_ref.shape[0]
    feat_base = small
    bias_base = small + features
    out_row = bias_base + layers + 1

    def as_col(block):
        spread = jnp.where(eye[None], block[:, None, :], 0.0)
        return jnp.sum(spread, axis=2, keepdims=True).reshape(CHUNK, 1)

    def body(k, carry):
        at = pl.multiple_of(k * per, per)
        row = pl.multiple_of(k * CHUNK, CHUNK)
        rho_col = as_col(rho_scr[pl.ds(at, per), :])
        quad_col = as_col(quad_scr[pl.ds(at, per), :])
        pre = pre_ref[pl.ds(row, CHUNK), :] + rho_col * win_ref[0:1, :]
        acts = [jnp.tanh(pre).astype(BF16)]
        for l in range(layers):
            inner = jnp.dot(acts[-1], wl_ref[l], preferred_element_type=F32)
            acts.append(jnp.tanh(inner + bias_ref[l + 1 : l + 2, :]).astype(BF16))
        top = acts[-1].astype(F32)
        score = jnp.sum(top * wout_ref[...], axis=1, keepdims=True)
        enhance = 2.0 * jax.nn.sigmoid(score)
        grad_score = quad_col * rho_col * enhance * (1.0 - 0.5 * enhance)
        grads_ref[out_row : out_row + 1, :] += jnp.sum(grad_score * top, axis=0, keepdims=True)
        grad = grad_score * wout_ref[...]
        for l in reversed(range(layers)):
            after = acts[l + 1].astype(F32)
            grad = grad * (1.0 - after * after)
            rounded = grad.astype(BF16)
            grads_ref[l * hidden : (l + 1) * hidden, :] += col_dot(acts[l], rounded)
            b = bias_base + l + 1
            grads_ref[b : b + 1, :] += jnp.sum(grad, axis=0, keepdims=True)
            grad = lax.dot_general(
                rounded, wl_ref[l], (((1,), (1,)), ((), ())), preferred_element_type=F32
            )
        first = acts[0].astype(F32)
        grad = grad * (1.0 - first * first)
        grads_ref[bias_base : bias_base + 1, :] += jnp.sum(grad, axis=0, keepdims=True)
        grads_ref[feat_base : feat_base + 1, :] += jnp.sum(grad * rho_col, axis=0, keepdims=True)
        hi = grad.astype(BF16)
        lo = (grad - hi.astype(F32)).astype(BF16)
        feat = feat_ref[:, pl.ds(row, CHUNK)]
        fhi = feat.astype(BF16)
        flo = (feat - fhi.astype(F32)).astype(BF16)
        term = (
            jnp.dot(fhi, hi, preferred_element_type=F32)
            + jnp.dot(fhi, lo, preferred_element_type=F32)
            + jnp.dot(flo, hi, preferred_element_type=F32)
        )
        grads_ref[feat_base + 1 : feat_base + features, :] += term[1:features]
        grad_rho = jnp.sum(grad * win_ref[0:1, :], axis=1, keepdims=True)
        weight = (quad_col * enhance + grad_rho).reshape(per, points, 1)
        pw_scr[pl.ds(at, per), :] = jnp.sum(jnp.where(eye[None], weight, 0.0), axis=1)
        return carry

    lax.fori_loop(0, batches // per, body, 0)
    batch_no = lax.broadcasted_iota(jnp.int32, (slots, batches), 1)
    back = (batch_no == src_ref[...]).astype(F32)
    sendw_ref[...] = jnp.dot(back, pw_scr[...], precision=highest, preferred_element_type=F32)


def potential_kernel(cap, pid_ref, ao_ref, w_ref, out_ref, acc_ref):
    sources = ao_ref.shape[0]
    points, width = ao_ref.shape[3:]
    me = lax.axis_index("wide")
    eye = eye_mask(points)
    acc_ref[...] = jnp.zeros_like(acc_ref)

    def body(i, own):
        w = w_ref[i]
        xs, ws = [], []
        for r in range(cap):
            x = ao_ref[i, r, 0]
            col = jnp.sum(jnp.where(eye, w[r : r + 1, :], 0.0), axis=1, keepdims=True)
            xs.append(x)
            ws.append((x.astype(F32) * col).astype(BF16))
        for r in range(cap):
            c = pid_ref[i, r]
            acc_ref[c] += col_dot(ws[r], ao_ref[i, r, 1])
        return own + col_dot(jnp.concatenate(ws, axis=0), jnp.concatenate(xs, axis=0))

    own = lax.fori_loop(0, sources, body, jnp.zeros((width, width), F32))
    acc_ref[me] += own
    for c in range(acc_ref.shape[0]):
        out_ref[:, c * width : (c + 1) * width] = acc_ref[c].astype(out_ref.dtype)


def shards(
    density, ao_values, block_lists, counts, other_features, quad_weights, w_in, biases, w_layers,
    w_out,
):
    n = lax.axis_size("wide")
    batches, entries, points, width = ao_values.shape
    blocks = density.shape[1] // width
    cap = max(2, (batches * entries + blocks - 1) // blocks)
    capp = up8(cap)
    hidden = w_out.shape[0]
    layers = w_layers.shape[0]
    features = w_in.shape[0]
    total = batches * entries
    live = jnp.arange(entries)[None, :] < counts[:, None]
    masked = jnp.where(live[:, :, None, None], ao_values, jnp.zeros((), ao_values.dtype))
    masked = masked.reshape(total, points, width)
    target = block_lists.reshape(-1)
    ids = jnp.arange(total, dtype=jnp.int32)
    earlier = (target[:, None] == target[None, :]) & (ids[None, :] < ids[:, None])
    rank = jnp.sum(earlier.astype(jnp.int32), axis=1)
    slot_of = target * cap + rank
    table = slot_of[None, :] == jnp.arange(n * cap, dtype=jnp.int32)[:, None]
    filled = jnp.any(table, axis=1)
    source = jnp.sum(jnp.where(table, ids[None, :], 0), axis=1)
    partner = jnp.sum(
        jnp.where(table, jnp.flip(block_lists, 1).reshape(-1)[None, :], 0), axis=1
    )
    pairs = jnp.stack([source, source ^ 1], axis=1)
    send_ao = jnp.where(filled[:, None, None, None], masked[pairs], jnp.zeros((), masked.dtype))
    send_ao = send_ao.reshape(n, cap, 2, points, width)
    a2a = functools.partial(
        lax.all_to_all, axis_name="wide", split_axis=0, concat_axis=0, tiled=True
    )
    recv_ao = a2a(send_ao)
    recv_pid = a2a(partner.reshape(n, cap))
    parts = pl.pallas_call(
        functools.partial(rho_kernel, cap),
        out_shape=jax.ShapeDtypeStruct((n, capp, 128), F32),
        in_specs=[SMEM, VMEM, VMEM],
        out_specs=VMEM,
        compiler_params=PARAMS,
    )(recv_pid, recv_ao, density)
    returned = a2a(parts)
    rows = batches * points
    pre_other = (
        jnp.einsum("bfp,fh->bph", other_features, w_in[1:], precision=highest) + biases[0]
    ).reshape(rows, hidden)
    feat = jnp.concatenate(
        [
            jnp.zeros((1, rows), F32),
            other_features.transpose(1, 0, 2).reshape(features - 1, rows),
        ],
        axis=0,
    )
    slot_pad = (target * capp + rank).reshape(batches, entries)
    src_pad = jnp.where(filled, source // entries, -1).reshape(n, cap)
    src_pad = jnp.pad(src_pad, ((0, 0), (0, capp - cap)), constant_values=-1).reshape(n * capp, 1)
    grad_rows = up8(layers * hidden + features + layers + 2)
    send_w, grads = pl.pallas_call(
        mlp_kernel,
        out_shape=(
            jax.ShapeDtypeStruct((n * capp, 128), F32),
            jax.ShapeDtypeStruct((grad_rows, hidden), F32),
        ),
        in_specs=[VMEM] * 10,
        out_specs=(VMEM, VMEM),
        scratch_shapes=[pltpu.VMEM((batches, 128), F32)] * 3,
        compiler_params=PARAMS,
    )(
        slot_pad, src_pad, returned.reshape(n * capp, 128), pre_other, feat, quad_weights, w_in,
        biases, w_layers, w_out[None, :],
    )
    recv_w = a2a(send_w.reshape(n, capp, 128))
    grads = lax.psum(grads, "wide")
    potential = pl.pallas_call(
        functools.partial(potential_kernel, cap),
        out_shape=jax.ShapeDtypeStruct(density.shape, density.dtype),
        in_specs=[SMEM, VMEM, VMEM],
        out_specs=VMEM,
        scratch_shapes=[pltpu.VMEM((blocks, width, width), F32)],
        compiler_params=PARAMS,
    )(recv_pid, recv_ao, recv_w)
    base = layers * hidden
    return (
        potential,
        grads[:base].reshape(layers, hidden, hidden),
        grads[base : base + features],
        grads[base + features : base + features + layers + 1],
        grads[base + features + layers + 1],
    )


def solution(mesh):
    placed = (
        P(("groups", "wide"), None),
        P(("groups", "wide"), None, None, None),
        P(("groups", "wide"), None),
        P(("groups", "wide")),
        P(("groups", "wide"), None, None),
        P(("groups", "wide"), None),
        P(),
        P(),
        P(),
        P(),
    )
    return jax.shard_map(
        shards,
        mesh=mesh,
        in_specs=placed,
        out_specs=(
            P(("groups", "wide"), None),
            P("groups", None, None),
            P("groups", None),
            P("groups", None),
            P("groups"),
        ),
        check_vma=False,
    )
```

```python
import functools

import jax
import jax.numpy as jnp
from jax import lax
from jax.experimental import pallas as pl
from jax.experimental.pallas import tpu as pltpu
from jax.sharding import PartitionSpec as P

highest = lax.Precision.HIGHEST
F32 = jnp.float32
BF16 = jnp.bfloat16
CHUNK = 512
VMEM = pl.BlockSpec(memory_space=pltpu.VMEM)
SMEM = pl.BlockSpec(memory_space=pltpu.SMEM)


def up8(x):
    return (x + 7) // 8 * 8


def eye_mask(points):
    return lax.broadcasted_iota(jnp.int32, (points, 128), 0) == lax.broadcasted_iota(
        jnp.int32, (points, 128), 1
    )


def col_dot(a, b):
    return lax.dot_general(a, b, (((0,), (0,)), ((), ())), preferred_element_type=F32)


def fused_kernel(
    cap, chunk_rows,
    src_ref, mate_ref, lo_ref, lp_ref, pidmsg_ref, ao_ref, den_ref, slot_ref, srcpad_ref, feat_ref, quad_ref,
    win_ref, bias_ref, wl_ref, wout_ref,
    pot_ref, gw_ref, gin_ref, gbias_ref, gout_ref,
    send_ao, recv_ao, recv_pid, table, stable, send_part, ret, pre_scr, rho_scr, quad_scr, pw_scr,
    small, grads, send_w, recv_w, send_g, recv_g, send_a, recv_a, send_s, recv_s, prefix, den,
    ssem, rsem, tsem,
):
    n = send_part.shape[0]
    points, width = ao_ref.shape[1:]
    batches = quad_ref.shape[0]
    hidden = wout_ref.shape[1]
    layers = wl_ref.shape[0]
    features = feat_ref.shape[0]
    halves = hidden // 128
    slots = n * cap
    capp = send_part.shape[1]
    blocks = den_ref.shape[1] // width
    me = lax.axis_index("wide")
    eye = eye_mask(points)

    def peer(d):
        return lax.rem(me + d, n)

    def origin(d):
        return lax.rem(me + n - d, n)

    def mine(k):
        return pl.ds(k * cap, cap)

    def copy(phase, src, dst, d):
        return pltpu.make_async_remote_copy(
            src_ref=src, dst_ref=dst, send_sem=ssem.at[phase, d], recv_sem=rsem.at[phase, d],
            device_id={"wide": peer(d)}, device_id_type=pl.DeviceIdType.MESH,
        )

    def each(fn):
        def body(d, carry):
            fn(d)
            return carry

        lax.fori_loop(1, n, body, 0)

    barrier = pltpu.get_barrier_semaphore()

    def greet(d):
        pl.semaphore_signal(
            barrier, inc=1, device_id={"wide": peer(d)}, device_id_type=pl.DeviceIdType.MESH
        )

    each(greet)

    def fill(k):
        for r in range(cap):
            e = src_ref[k, r]
            own = ao_ref[e].astype(F32) * lo_ref[k, r].astype(F32)
            mate = mate_ref[k, r]
            other = ao_ref[mate].astype(F32) * lp_ref[k, r].astype(F32)
            send_ao[k * cap + r, 0] = own.astype(BF16)
            send_ao[k * cap + r, 1] = other.astype(BF16)

    def pid_copy(d):
        return copy(0, pidmsg_ref.at[peer(d)], recv_pid.at[me], d)

    def pid_back(d):
        return copy(0, pidmsg_ref.at[peer(d)], recv_pid.at[origin(d)], d)

    def ao_copy(d):
        return copy(1, send_ao.at[mine(peer(d))], recv_ao.at[mine(me)], d)

    def ao_back(d):
        return copy(1, send_ao.at[mine(peer(d))], recv_ao.at[mine(origin(d))], d)

    pl.semaphore_wait(barrier, n - 1)
    each(lambda d: pid_copy(d).start())

    def send_one(d):
        fill(peer(d))
        ao_copy(d).start()

    each(send_one)
    fill(me)
    recv_ao[mine(me)] = send_ao[mine(me)]
    recv_pid[me] = pidmsg_ref[me]

    def den_body(c, carry):
        den[c] = den_ref[:, pl.ds(pl.multiple_of(c * width, width), width)]
        return carry

    lax.fori_loop(0, blocks, den_body, 0)
    per = CHUNK // points
    quad_scr[...] = jnp.zeros_like(quad_scr)
    quad_scr[:, 0:points] = quad_ref[...]
    grads[...] = jnp.zeros_like(grads)
    small[...] = jnp.zeros_like(small)

    def pre_body(k, carry):
        row = pl.multiple_of(k * CHUNK, CHUNK)
        part = lax.dot_general(
            feat_ref[:, pl.ds(row, CHUNK)], win_ref[...], (((0,), (0,)), ((), ())),
            precision=highest, preferred_element_type=F32,
        )
        pre_scr[pl.ds(row, CHUNK), :] = part + bias_ref[0:1, :]
        return carry

    lax.fori_loop(0, batches // per, pre_body, 0)

    each(lambda d: pid_back(d).wait_recv())
    pid_row = lax.fori_loop(
        0, n, lambda i, a: a + recv_pid[i], jnp.zeros(recv_pid.shape[1:], jnp.int32)
    )[0:1, :]
    up = lax.broadcasted_iota(jnp.int32, (slots, slots), 0)
    across = lax.broadcasted_iota(jnp.int32, (slots, slots), 1)
    pid_col = jnp.sum(jnp.where(up == across, pid_row, 0), axis=1, keepdims=True)
    twin = (pid_row == pid_col) & (across < up)
    order = jnp.sum(((pid_row < pid_col) | twin).astype(jnp.int32), axis=1, keepdims=True)
    held = jnp.max(twin.astype(jnp.int32), axis=1, keepdims=True)
    placed = order == across
    table[...] = jnp.zeros_like(table)
    table[0:1, :] = pid_row
    table[1:2, :] = jnp.sum(jnp.where(placed, up, 0), axis=0, keepdims=True)
    table[2:3, :] = jnp.sum(jnp.where(placed, held, 0), axis=0, keepdims=True)
    upto = jnp.sum((pid_col <= across).astype(jnp.int32), axis=0, keepdims=True)
    table[3:4, :] = jnp.maximum(upto - 1, 0)
    table[4:5, :] = jnp.max((pid_col == across).astype(jnp.int32), axis=0, keepdims=True)
    to_scalar = pltpu.make_async_copy(table, stable, tsem.at[0])
    to_scalar.start()
    to_scalar.wait()

    own = den[me]

    def shares(i):
        rows = []
        for r in range(cap):
            c = stable[0, i * cap + r]
            other = den[c]
            x = recv_ao[i * cap + r, 0]
            y = recv_ao[i * cap + r, 1]
            q = jnp.dot(x, own, preferred_element_type=F32) * x.astype(F32)
            q = q + jnp.dot(x, other, preferred_element_type=F32) * y.astype(F32)
            col = jnp.sum(q, axis=1, keepdims=True)
            rows.append(jnp.sum(jnp.where(eye, col, 0.0), axis=0, keepdims=True))
        if capp > cap:
            rows.append(jnp.zeros((capp - cap, 128), F32))
        return jnp.concatenate(rows, axis=0)

    def part_copy(d):
        return copy(2, send_part.at[peer(d)], ret.at[me], d)

    def part_back(d):
        return copy(2, send_part.at[peer(d)], ret.at[origin(d)], d)

    ret[me] = shares(me)

    def answer(d):
        src = origin(d)
        ao_back(d).wait_recv()
        send_part[src] = shares(src)
        copy(2, send_part.at[src], ret.at[me], n - d).start()

    each(answer)
    each(lambda d: part_back(d).wait_recv())

    slot_no = lax.broadcasted_iota(jnp.int32, (batches, n * capp), 1)
    pick = (slot_no == slot_ref[:, 0:1]) | (slot_no == slot_ref[:, 1:2])
    rho_scr[...] = jnp.dot(
        pick.astype(F32), ret[...].reshape(n * capp, 128), precision=highest,
        preferred_element_type=F32,
    )
    bias_base = features
    out_row = bias_base + layers + 1

    def as_col(block):
        spread = jnp.where(eye[None], block[:, None, :], 0.0)
        return jnp.sum(spread, axis=2, keepdims=True).reshape(CHUNK, 1)

    def body(k, carry):
        at = pl.multiple_of(k * per, per)
        row = pl.multiple_of(k * CHUNK, CHUNK)
        rho_col = as_col(rho_scr[pl.ds(at, per), :])
        quad_col = as_col(quad_scr[pl.ds(at, per), :])
        pre = pre_scr[pl.ds(row, CHUNK), :] + rho_col * win_ref[0:1, :]
        acts = [jnp.tanh(pre).astype(BF16)]
        for l in range(layers):
            inner = jnp.dot(acts[-1], wl_ref[l], preferred_element_type=F32)
            acts.append(jnp.tanh(inner + bias_ref[l + 1 : l + 2, :]).astype(BF16))
        top = acts[-1].astype(F32)
        score = jnp.sum(top * wout_ref[...], axis=1, keepdims=True)
        enhance = 2.0 * jax.nn.sigmoid(score)
        grad_score = quad_col * rho_col * enhance * (1.0 - 0.5 * enhance)
        small[out_row : out_row + 1, :] += jnp.sum(grad_score * top, axis=0, keepdims=True)
        grad = grad_score * wout_ref[...]
        for l in reversed(range(layers)):
            after = acts[l + 1].astype(F32)
            grad = grad * (1.0 - after * after)
            rounded = grad.astype(BF16)
            grads[l * hidden : (l + 1) * hidden, :] += col_dot(acts[l], rounded)
            b = bias_base + l + 1
            small[b : b + 1, :] += jnp.sum(grad, axis=0, keepdims=True)
            grad = lax.dot_general(
                rounded, wl_ref[l], (((1,), (1,)), ((), ())), preferred_element_type=F32
            )
        first = acts[0].astype(F32)
        grad = grad * (1.0 - first * first)
        small[bias_base : bias_base + 1, :] += jnp.sum(grad, axis=0, keepdims=True)
        small[0:1, :] += jnp.sum(grad * rho_col, axis=0, keepdims=True)
        hi = grad.astype(BF16)
        lo = (grad - hi.astype(F32)).astype(BF16)
        feat = feat_ref[:, pl.ds(row, CHUNK)]
        fhi = feat.astype(BF16)
        flo = (feat - fhi.astype(F32)).astype(BF16)
        term = (
            jnp.dot(fhi, hi, preferred_element_type=F32)
            + jnp.dot(fhi, lo, preferred_element_type=F32)
            + jnp.dot(flo, hi, preferred_element_type=F32)
        )
        small[1:features, :] += term[1:features]
        grad_rho = jnp.sum(grad * win_ref[0:1, :], axis=1, keepdims=True)
        weight = (quad_col * enhance + grad_rho).reshape(per, points, 1)
        pw_scr[pl.ds(at, per), :] = jnp.sum(jnp.where(eye[None], weight, 0.0), axis=1)
        return carry

    lax.fori_loop(0, batches // per, body, 0)
    batch_no = lax.broadcasted_iota(jnp.int32, (n * capp, batches), 1)
    back = (batch_no == srcpad_ref[...]).astype(F32)
    send_w[:, capp:, :] = jnp.zeros((n, 8, 128), F32)
    send_w[:, 0:capp, :] = jnp.dot(
        back, pw_scr[...], precision=highest, preferred_element_type=F32
    ).reshape(n, capp, 128)
    small_rows = out_row + 1
    for k in range(small_rows):
        for h in range(halves):
            send_w[k, capp + h : capp + h + 1, :] = small[k : k + 1, h * 128 : (h + 1) * 128]

    def w_copy(d):
        return copy(3, send_w.at[peer(d)], recv_w.at[me], d)

    def w_back(d):
        return copy(3, send_w.at[peer(d)], recv_w.at[origin(d)], d)

    def g_copy(d):
        return copy(4, send_g.at[peer(d)], recv_g.at[me], d)

    def g_back(d):
        return copy(4, send_g.at[peer(d)], recv_g.at[origin(d)], d)

    def a_copy(d):
        return copy(5, send_a, recv_a.at[me], d)

    def a_back(d):
        return copy(5, send_a, recv_a.at[origin(d)], d)

    def s_copy(d):
        return copy(6, send_s, recv_s.at[me], d)

    def s_back(d):
        return copy(6, send_s, recv_s.at[origin(d)], d)

    each(lambda d: w_copy(d).start())

    def send_grad(d):
        k = peer(d)
        at = pl.multiple_of(k * chunk_rows, 16)
        send_g[k] = grads[pl.ds(at, chunk_rows), :].astype(BF16)
        g_copy(d).start()

    each(send_grad)
    recv_w[me] = send_w[me]
    each(lambda d: w_back(d).wait_recv())
    send_s[...] = lax.fori_loop(
        0, n, lambda i, a: a + recv_w[i, capp:, :], jnp.zeros((8, 128), F32)
    )
    each(lambda d: s_copy(d).start())

    def own_body(i, acc):
        w = recv_w[i]
        xs, ws = [], []
        for r in range(cap):
            x = recv_ao[i * cap + r, 0]
            col = jnp.sum(jnp.where(eye, w[r : r + 1, :], 0.0), axis=1, keepdims=True)
            weighted = (x.astype(F32) * col).astype(BF16)
            send_ao[i * cap + r, 0] = weighted
            xs.append(x)
            ws.append(weighted)
        return acc + col_dot(jnp.concatenate(ws, axis=0), jnp.concatenate(xs, axis=0))

    each(lambda d: ao_copy(d).wait_send())
    own_sum = lax.fori_loop(0, n, own_body, jnp.zeros((width, width), F32))
    group = 8

    def sorted_body(g, acc):
        for u in range(group):
            j = g * group + u
            s = stable[1, j]
            part = col_dot(send_ao[s, 0], recv_ao[s, 1])
            acc = acc * stable[2, j].astype(F32) + part
            prefix[j] = acc
        return acc

    lax.fori_loop(0, slots // group, sorted_body, jnp.zeros((width, width), F32))

    at = pl.multiple_of(me * chunk_rows, 16)
    each(lambda d: g_back(d).wait_recv())
    total = grads[pl.ds(at, chunk_rows), :]
    recv_g[me] = jnp.zeros(recv_g.shape[1:], BF16)
    total = lax.fori_loop(0, n, lambda i, a: a + recv_g[i].astype(F32), total)
    send_a[...] = total.astype(BF16)
    each(lambda d: a_copy(d).start())

    def out_body(c, carry):
        end = stable[3, c]
        value = prefix[end] * stable[4, c].astype(F32)
        value = value + own_sum * (c == me).astype(F32)
        pot_ref[:, pl.ds(pl.multiple_of(c * width, width), width)] = value.astype(pot_ref.dtype)
        return carry

    lax.fori_loop(0, blocks, out_body, 0)
    recv_a[me] = send_a[...]
    recv_s[me] = send_s[...]
    each(lambda d: s_back(d).wait_recv())
    for k in range(small_rows):
        row = jnp.concatenate([recv_s[k, h : h + 1, :] for h in range(halves)], axis=1)
        if k < features:
            gin_ref[k : k + 1, :] = row
        elif k < out_row:
            gbias_ref[k - features : k - features + 1, :] = row
        else:
            gout_ref[...] = row
    each(lambda d: a_back(d).wait_recv())

    def gw_body(k, carry):
        at = pl.multiple_of(k * chunk_rows, 16)
        gw_ref[pl.ds(at, chunk_rows), :] = recv_a[k].astype(F32)
        return carry

    lax.fori_loop(0, layers * hidden // chunk_rows, gw_body, 0)

    def drain(d):
        pid_copy(d).wait_send()
        part_copy(d).wait_send()
        w_copy(d).wait_send()
        g_copy(d).wait_send()
        a_copy(d).wait_send()
        s_copy(d).wait_send()

    each(drain)


def shards(
    density, ao_values, block_lists, counts, other_features, quad_weights, w_in, biases, w_layers,
    w_out,
):
    n = lax.axis_size("wide")
    me = lax.axis_index("wide")
    batches, entries, points, width = ao_values.shape
    blocks = density.shape[1] // width
    cap = max(2, (batches * entries + blocks - 1) // blocks)
    capp = up8(cap)
    slots = n * cap
    hidden = w_out.shape[0]
    layers = w_layers.shape[0]
    features = w_in.shape[0]
    total = batches * entries
    rows = batches * points
    target = block_lists.reshape(-1)
    ids = jnp.arange(total, dtype=jnp.int32)
    earlier = (target[:, None] == target[None, :]) & (ids[None, :] < ids[:, None])
    rank = jnp.sum(earlier.astype(jnp.int32), axis=1)
    slot_of = target * cap + rank
    table = slot_of[None, :] == jnp.arange(slots, dtype=jnp.int32)[:, None]
    live = (jnp.arange(entries)[None, :] < counts[:, None]).astype(jnp.int32)

    def at_slot(values):
        return jnp.sum(jnp.where(table, values.reshape(-1)[None, :], 0), axis=1).reshape(n, cap)

    source = at_slot(ids)
    partner = at_slot(jnp.flip(block_lists, 1))
    live_own = at_slot(live)
    live_other = at_slot(jnp.flip(live, 1))
    filled = jnp.any(table, axis=1).reshape(n, cap)
    lane = jnp.arange(slots, dtype=jnp.int32)
    spread = jnp.where(lane[None, :] // cap == me, jnp.tile(partner, (1, n)), 0)
    pid_msg = jnp.broadcast_to(spread[:, None, :], (n, 8, slots))
    feat = jnp.concatenate(
        [
            jnp.zeros((1, rows), F32),
            other_features.transpose(1, 0, 2).reshape(features - 1, rows),
        ],
        axis=0,
    )
    slot_pad = (target * capp + rank).reshape(batches, entries)
    src_pad = jnp.where(filled, source // entries, -1)
    src_pad = jnp.pad(src_pad, ((0, 0), (0, capp - cap)), constant_values=-1).reshape(n * capp, 1)
    weight_rows = layers * hidden
    chunk_rows = (-(-weight_rows // n) + 15) // 16 * 16
    while weight_rows % chunk_rows:
        chunk_rows += 16
    small_rows = up8(features + layers + 2)
    vm = pltpu.VMEM
    potential, gw, gin, gbias, gout = pl.pallas_call(
        functools.partial(fused_kernel, cap, chunk_rows),
        out_shape=(
            jax.ShapeDtypeStruct(density.shape, density.dtype),
            jax.ShapeDtypeStruct((weight_rows, hidden), F32),
            jax.ShapeDtypeStruct((features, hidden), F32),
            jax.ShapeDtypeStruct((layers + 1, hidden), F32),
            jax.ShapeDtypeStruct((1, hidden), F32),
        ),
        in_specs=[SMEM] * 4 + [VMEM] * 11,
        out_specs=(VMEM,) * 5,
        scratch_shapes=[
            vm((slots, 2, points, width), BF16),
            vm((slots, 2, points, width), BF16),
            vm((n, 8, slots), jnp.int32),
            vm((8, slots), jnp.int32),
            pltpu.SMEM((8, slots), jnp.int32),
            vm((n, capp, 128), F32),
            vm((n, capp, 128), F32),
            vm((rows, hidden), F32),
            vm((batches, 128), F32),
            vm((batches, 128), F32),
            vm((batches, 128), F32),
            vm((small_rows, hidden), F32),
            vm((n * chunk_rows, hidden), F32),
            vm((n, capp + 8, 128), F32),
            vm((n, capp + 8, 128), F32),
            vm((n, chunk_rows, hidden), BF16),
            vm((n, chunk_rows, hidden), BF16),
            vm((chunk_rows, hidden), BF16),
            vm((n, chunk_rows, hidden), BF16),
            vm((8, 128), F32),
            vm((n, 8, 128), F32),
            vm((slots, width, width), F32),
            vm((blocks, width, width), BF16),
            pltpu.SemaphoreType.DMA((7, n)),
            pltpu.SemaphoreType.DMA((7, n)),
            pltpu.SemaphoreType.DMA((1,)),
        ],
        compiler_params=pltpu.CompilerParams(
            vmem_limit_bytes=56 * 1024 * 1024, collective_id=0, has_side_effects=True
        ),
    )(
        source, source ^ 1, live_own, live_other, pid_msg, ao_values.reshape(total, points, width), density,
        slot_pad, src_pad, feat, quad_weights, w_in, biases, w_layers, w_out[None, :],
    )
    return (potential, gw.reshape(layers, hidden, hidden), gin, gbias, gout.reshape(hidden))


def solution(mesh):
    placed = (
        P(("groups", "wide"), None),
        P(("groups", "wide"), None, None, None),
        P(("groups", "wide"), None),
        P(("groups", "wide")),
        P(("groups", "wide"), None, None),
        P(("groups", "wide"), None),
        P(),
        P(),
        P(),
        P(),
    )
    return jax.shard_map(
        shards,
        mesh=mesh,
        in_specs=placed,
        out_specs=(
            P(("groups", "wide"), None),
            P("groups", None, None),
            P("groups", None),
            P("groups", None),
            P("groups"),
        ),
        check_vma=False,
    )
```

```python
import functools

import jax
import jax.numpy as jnp
from jax import lax
from jax.experimental import pallas as pl
from jax.experimental.pallas import tpu as pltpu
from jax.sharding import PartitionSpec as P

highest = lax.Precision.HIGHEST
F32 = jnp.float32
BF16 = jnp.bfloat16
CHUNK = 512
VMEM = pl.BlockSpec(memory_space=pltpu.VMEM)
SMEM = pl.BlockSpec(memory_space=pltpu.SMEM)


def up8(x):
    return (x + 7) // 8 * 8


def eye_mask(points):
    return lax.broadcasted_iota(jnp.int32, (points, 128), 0) == lax.broadcasted_iota(
        jnp.int32, (points, 128), 1
    )


def col_dot(a, b):
    return lax.dot_general(a, b, (((0,), (0,)), ((), ())), preferred_element_type=F32)


def fused_kernel(
    cap, chunk_rows,
    list_ref, count_ref, ao_ref, den_ref, feat_ref, quad_ref,
    win_ref, bias_ref, wl_ref, wout_ref,
    pot_ref, gw_ref, gin_ref, gbias_ref, gout_ref,
    send_ao, recv_ao, pid_msg, recv_pid, table, plan, splan, pick_scr, stable, send_part, ret, pre_scr, rho_scr, quad_scr, pw_scr,
    small, grads, send_w, recv_w, send_g, recv_g, send_a, recv_a, send_s, recv_s, prefix, den,
    ssem, rsem, tsem,
):
    n = send_part.shape[0]
    points, width = ao_ref.shape[1:]
    batches = quad_ref.shape[0]
    hidden = wout_ref.shape[1]
    layers = wl_ref.shape[0]
    features = feat_ref.shape[0]
    halves = hidden // 128
    slots = n * cap
    capp = send_part.shape[1]
    blocks = den_ref.shape[1] // width
    me = lax.axis_index("wide")
    eye = eye_mask(points)

    def peer(d):
        return lax.rem(me + d, n)

    def origin(d):
        return lax.rem(me + n - d, n)

    def mine(k):
        return pl.ds(k * cap, cap)

    def copy(phase, src, dst, d):
        return pltpu.make_async_remote_copy(
            src_ref=src, dst_ref=dst, send_sem=ssem.at[phase, d], recv_sem=rsem.at[phase, d],
            device_id={"wide": peer(d)}, device_id_type=pl.DeviceIdType.MESH,
        )

    def each(fn):
        def body(d, carry):
            fn(d)
            return carry

        lax.fori_loop(1, n, body, 0)

    barrier = pltpu.get_barrier_semaphore()

    def greet(d):
        pl.semaphore_signal(
            barrier, inc=1, device_id={"wide": peer(d)}, device_id_type=pl.DeviceIdType.MESH
        )

    each(greet)
    total = batches * 2
    up = lax.broadcasted_iota(jnp.int32, (total, total), 0)
    across = lax.broadcasted_iota(jnp.int32, (total, total), 1)
    first_ids = list_ref[:, 0:1]
    second_ids = list_ref[:, 1:2]
    target = jnp.concatenate([first_ids, second_ids], axis=0)
    partner = jnp.concatenate([second_ids, first_ids], axis=0)
    target_row = jnp.sum(jnp.where(up == across, target, 0), axis=0, keepdims=True)
    earlier = (target_row == target) & (across < up)
    rank = jnp.sum(earlier.astype(jnp.int32), axis=1, keepdims=True)
    square = (batches, batches)
    same = lax.broadcasted_iota(jnp.int32, square, 0) == lax.broadcasted_iota(jnp.int32, square, 1)
    used = jnp.sum(jnp.where(same, count_ref[...], 0), axis=1, keepdims=True)
    used = jnp.concatenate([used, used], axis=0)
    entry = lax.broadcasted_iota(jnp.int32, (total, 1), 0)
    second = (entry >= batches).astype(jnp.int32)
    source = 2 * (entry - batches * second) + second
    mate_entry = source + 1 - 2 * second
    slot_no = lax.broadcasted_iota(jnp.int32, (total, slots), 1)
    sits = slot_no == target * cap + rank

    def at_slot(values):
        return jnp.sum(jnp.where(sits, values, 0), axis=0, keepdims=True)

    plan[...] = jnp.zeros_like(plan)
    plan[0:1, :] = at_slot(source)
    plan[1:2, :] = at_slot(mate_entry)
    plan[2:3, :] = at_slot((second < used).astype(jnp.int32))
    plan[3:4, :] = at_slot((1 - second < used).astype(jnp.int32))
    pid_msg[...] = jnp.broadcast_to(at_slot(partner), pid_msg.shape)
    to_plan = pltpu.make_async_copy(plan, splan, tsem.at[1])
    to_plan.start()
    padded = lax.broadcasted_iota(jnp.int32, (batches, n * capp), 1)
    home = target * capp + rank
    pick = (padded == home[0:batches]) | (padded == home[batches:total])
    pick_scr[...] = pick.astype(F32)
    to_plan.wait()

    def fill(k):
        for r in range(cap):
            at = k * cap + r
            e = splan[0, at]
            own = ao_ref[e].astype(F32) * splan[2, at].astype(F32)
            mate = splan[1, at]
            other = ao_ref[mate].astype(F32) * splan[3, at].astype(F32)
            send_ao[k * cap + r, 0] = own.astype(BF16)
            send_ao[k * cap + r, 1] = other.astype(BF16)

    def pid_copy(d):
        return copy(0, pid_msg, recv_pid.at[me], d)

    def pid_back(d):
        return copy(0, pid_msg, recv_pid.at[origin(d)], d)

    def ao_copy(d):
        return copy(1, send_ao.at[mine(peer(d))], recv_ao.at[mine(me)], d)

    def ao_back(d):
        return copy(1, send_ao.at[mine(peer(d))], recv_ao.at[mine(origin(d))], d)

    pl.semaphore_wait(barrier, n - 1)
    each(lambda d: pid_copy(d).start())

    def send_one(d):
        fill(peer(d))
        ao_copy(d).start()

    each(send_one)
    fill(me)
    recv_ao[mine(me)] = send_ao[mine(me)]
    recv_pid[me] = pid_msg[...]

    def den_body(c, carry):
        den[c] = den_ref[:, pl.ds(pl.multiple_of(c * width, width), width)]
        return carry

    lax.fori_loop(0, blocks, den_body, 0)
    per = CHUNK // points
    quad_scr[...] = jnp.zeros_like(quad_scr)
    quad_scr[:, 0:points] = quad_ref[...]
    grads[...] = jnp.zeros_like(grads)
    small[...] = jnp.zeros_like(small)

    def pre_body(k, carry):
        row = pl.multiple_of(k * CHUNK, CHUNK)
        part = lax.dot_general(
            feat_ref[:, pl.ds(row, CHUNK)], win_ref[...], (((0,), (0,)), ((), ())),
            precision=highest, preferred_element_type=F32,
        )
        pre_scr[pl.ds(row, CHUNK), :] = part + bias_ref[0:1, :]
        return carry

    lax.fori_loop(0, batches // per, pre_body, 0)

    each(lambda d: pid_back(d).wait_recv())
    lists = jnp.max(recv_pid[...], axis=1)
    lane = lax.broadcasted_iota(jnp.int32, (n, slots), 1)
    base = lax.broadcasted_iota(jnp.int32, (n, slots), 0) * cap
    gathered = jnp.zeros((n, slots), jnp.int32)
    for r in range(cap):
        mine_r = jnp.sum(jnp.where(lane == me * cap + r, lists, 0), axis=1, keepdims=True)
        gathered = gathered + jnp.where(lane == base + r, mine_r, 0)
    pid_row = jnp.sum(gathered, axis=0, keepdims=True)
    up = lax.broadcasted_iota(jnp.int32, (slots, slots), 0)
    across = lax.broadcasted_iota(jnp.int32, (slots, slots), 1)
    pid_col = jnp.sum(jnp.where(up == across, pid_row, 0), axis=1, keepdims=True)
    twin = (pid_row == pid_col) & (across < up)
    order = jnp.sum(((pid_row < pid_col) | twin).astype(jnp.int32), axis=1, keepdims=True)
    held = jnp.max(twin.astype(jnp.int32), axis=1, keepdims=True)
    placed = order == across
    table[...] = jnp.zeros_like(table)
    table[0:1, :] = pid_row
    table[1:2, :] = jnp.sum(jnp.where(placed, up, 0), axis=0, keepdims=True)
    table[2:3, :] = jnp.sum(jnp.where(placed, held, 0), axis=0, keepdims=True)
    upto = jnp.sum((pid_col <= across).astype(jnp.int32), axis=0, keepdims=True)
    table[3:4, :] = jnp.maximum(upto - 1, 0)
    table[4:5, :] = jnp.max((pid_col == across).astype(jnp.int32), axis=0, keepdims=True)
    to_scalar = pltpu.make_async_copy(table, stable, tsem.at[0])
    to_scalar.start()
    to_scalar.wait()

    own = den[me]

    def shares(i):
        rows = []
        for r in range(cap):
            c = stable[0, i * cap + r]
            other = den[c]
            x = recv_ao[i * cap + r, 0]
            y = recv_ao[i * cap + r, 1]
            q = jnp.dot(x, own, preferred_element_type=F32) * x.astype(F32)
            q = q + jnp.dot(x, other, preferred_element_type=F32) * y.astype(F32)
            col = jnp.sum(q, axis=1, keepdims=True)
            rows.append(jnp.sum(jnp.where(eye, col, 0.0), axis=0, keepdims=True))
        if capp > cap:
            rows.append(jnp.zeros((capp - cap, 128), F32))
        return jnp.concatenate(rows, axis=0)

    def part_copy(d):
        return copy(2, send_part.at[peer(d)], ret.at[me], d)

    def part_back(d):
        return copy(2, send_part.at[peer(d)], ret.at[origin(d)], d)

    ret[me] = shares(me)

    def answer(d):
        src = origin(d)
        ao_back(d).wait_recv()
        send_part[src] = shares(src)
        copy(2, send_part.at[src], ret.at[me], n - d).start()

    each(answer)
    each(lambda d: part_back(d).wait_recv())

    rho_scr[...] = jnp.dot(
        pick_scr[...], ret[...].reshape(n * capp, 128), precision=highest,
        preferred_element_type=F32,
    )
    bias_base = features
    out_row = bias_base + layers + 1

    def as_col(block):
        spread = jnp.where(eye[None], block[:, None, :], 0.0)
        return jnp.sum(spread, axis=2, keepdims=True).reshape(CHUNK, 1)

    def body(k, carry):
        at = pl.multiple_of(k * per, per)
        row = pl.multiple_of(k * CHUNK, CHUNK)
        rho_col = as_col(rho_scr[pl.ds(at, per), :])
        quad_col = as_col(quad_scr[pl.ds(at, per), :])
        pre = pre_scr[pl.ds(row, CHUNK), :] + rho_col * win_ref[0:1, :]
        acts = [jnp.tanh(pre).astype(BF16)]
        for l in range(layers):
            inner = jnp.dot(acts[-1], wl_ref[l], preferred_element_type=F32)
            acts.append(jnp.tanh(inner + bias_ref[l + 1 : l + 2, :]).astype(BF16))
        top = acts[-1].astype(F32)
        score = jnp.sum(top * wout_ref[...], axis=1, keepdims=True)
        enhance = 2.0 * jax.nn.sigmoid(score)
        grad_score = quad_col * rho_col * enhance * (1.0 - 0.5 * enhance)
        small[out_row : out_row + 1, :] += jnp.sum(grad_score * top, axis=0, keepdims=True)
        grad = grad_score * wout_ref[...]
        for l in reversed(range(layers)):
            after = acts[l + 1].astype(F32)
            grad = grad * (1.0 - after * after)
            rounded = grad.astype(BF16)
            grads[l * hidden : (l + 1) * hidden, :] += col_dot(acts[l], rounded)
            b = bias_base + l + 1
            small[b : b + 1, :] += jnp.sum(grad, axis=0, keepdims=True)
            grad = lax.dot_general(
                rounded, wl_ref[l], (((1,), (1,)), ((), ())), preferred_element_type=F32
            )
        first = acts[0].astype(F32)
        grad = grad * (1.0 - first * first)
        small[bias_base : bias_base + 1, :] += jnp.sum(grad, axis=0, keepdims=True)
        small[0:1, :] += jnp.sum(grad * rho_col, axis=0, keepdims=True)
        hi = grad.astype(BF16)
        lo = (grad - hi.astype(F32)).astype(BF16)
        feat = feat_ref[:, pl.ds(row, CHUNK)]
        fhi = feat.astype(BF16)
        flo = (feat - fhi.astype(F32)).astype(BF16)
        term = (
            jnp.dot(fhi, hi, preferred_element_type=F32)
            + jnp.dot(fhi, lo, preferred_element_type=F32)
            + jnp.dot(flo, hi, preferred_element_type=F32)
        )
        small[1:features, :] += term[1:features]
        grad_rho = jnp.sum(grad * win_ref[0:1, :], axis=1, keepdims=True)
        weight = (quad_col * enhance + grad_rho).reshape(per, points, 1)
        pw_scr[pl.ds(at, per), :] = jnp.sum(jnp.where(eye[None], weight, 0.0), axis=1)
        return carry

    lax.fori_loop(0, batches // per, body, 0)
    send_w[:, capp:, :] = jnp.zeros((n, 8, 128), F32)
    send_w[:, 0:capp, :] = lax.dot_general(
        pick_scr[...], pw_scr[...], (((0,), (0,)), ((), ())), precision=highest,
        preferred_element_type=F32,
    ).reshape(n, capp, 128)
    small_rows = out_row + 1
    for k in range(small_rows):
        for h in range(halves):
            send_w[k, capp + h : capp + h + 1, :] = small[k : k + 1, h * 128 : (h + 1) * 128]

    def w_copy(d):
        return copy(3, send_w.at[peer(d)], recv_w.at[me], d)

    def w_back(d):
        return copy(3, send_w.at[peer(d)], recv_w.at[origin(d)], d)

    def g_copy(d):
        return copy(4, send_g.at[peer(d)], recv_g.at[me], d)

    def g_back(d):
        return copy(4, send_g.at[peer(d)], recv_g.at[origin(d)], d)

    def a_copy(d):
        return copy(5, send_a, recv_a.at[me], d)

    def a_back(d):
        return copy(5, send_a, recv_a.at[origin(d)], d)

    def s_copy(d):
        return copy(6, send_s, recv_s.at[me], d)

    def s_back(d):
        return copy(6, send_s, recv_s.at[origin(d)], d)

    each(lambda d: w_copy(d).start())

    def send_grad(d):
        k = peer(d)
        at = pl.multiple_of(k * chunk_rows, 16)
        send_g[k] = grads[pl.ds(at, chunk_rows), :].astype(BF16)
        g_copy(d).start()

    each(send_grad)
    recv_w[me] = send_w[me]
    each(lambda d: w_back(d).wait_recv())
    send_s[...] = lax.fori_loop(
        0, n, lambda i, a: a + recv_w[i, capp:, :], jnp.zeros((8, 128), F32)
    )
    each(lambda d: s_copy(d).start())

    def own_body(i, acc):
        w = recv_w[i]
        xs, ws = [], []
        for r in range(cap):
            x = recv_ao[i * cap + r, 0]
            col = jnp.sum(jnp.where(eye, w[r : r + 1, :], 0.0), axis=1, keepdims=True)
            weighted = (x.astype(F32) * col).astype(BF16)
            send_ao[i * cap + r, 0] = weighted
            xs.append(x)
            ws.append(weighted)
        return acc + col_dot(jnp.concatenate(ws, axis=0), jnp.concatenate(xs, axis=0))

    each(lambda d: ao_copy(d).wait_send())
    own_sum = lax.fori_loop(0, n, own_body, jnp.zeros((width, width), F32))
    group = 8

    def sorted_body(g, acc):
        for u in range(group):
            j = g * group + u
            s = stable[1, j]
            part = col_dot(send_ao[s, 0], recv_ao[s, 1])
            acc = acc * stable[2, j].astype(F32) + part
            prefix[j] = acc
        return acc

    lax.fori_loop(0, slots // group, sorted_body, jnp.zeros((width, width), F32))

    at = pl.multiple_of(me * chunk_rows, 16)
    each(lambda d: g_back(d).wait_recv())
    total = grads[pl.ds(at, chunk_rows), :]
    recv_g[me] = jnp.zeros(recv_g.shape[1:], BF16)
    total = lax.fori_loop(0, n, lambda i, a: a + recv_g[i].astype(F32), total)
    send_a[...] = total.astype(BF16)
    each(lambda d: a_copy(d).start())

    def out_body(c, carry):
        end = stable[3, c]
        value = prefix[end] * stable[4, c].astype(F32)
        value = value + own_sum * (c == me).astype(F32)
        pot_ref[:, pl.ds(pl.multiple_of(c * width, width), width)] = value.astype(pot_ref.dtype)
        return carry

    lax.fori_loop(0, blocks, out_body, 0)
    recv_a[me] = send_a[...]
    recv_s[me] = send_s[...]
    each(lambda d: s_back(d).wait_recv())
    for k in range(small_rows):
        row = jnp.concatenate([recv_s[k, h : h + 1, :] for h in range(halves)], axis=1)
        if k < features:
            gin_ref[k : k + 1, :] = row
        elif k < out_row:
            gbias_ref[k - features : k - features + 1, :] = row
        else:
            gout_ref[...] = row
    each(lambda d: a_back(d).wait_recv())

    def gw_body(k, carry):
        at = pl.multiple_of(k * chunk_rows, 16)
        gw_ref[pl.ds(at, chunk_rows), :] = recv_a[k].astype(F32)
        return carry

    lax.fori_loop(0, layers * hidden // chunk_rows, gw_body, 0)

    def drain(d):
        pid_copy(d).wait_send()
        part_copy(d).wait_send()
        w_copy(d).wait_send()
        g_copy(d).wait_send()
        a_copy(d).wait_send()
        s_copy(d).wait_send()

    each(drain)


def shards(
    density, ao_values, block_lists, counts, other_features, quad_weights, w_in, biases, w_layers,
    w_out,
):
    n = lax.axis_size("wide")
    batches, entries, points, width = ao_values.shape
    blocks = density.shape[1] // width
    cap = max(2, (batches * entries + blocks - 1) // blocks)
    capp = up8(cap)
    slots = n * cap
    hidden = w_out.shape[0]
    layers = w_layers.shape[0]
    features = w_in.shape[0]
    total = batches * entries
    rows = batches * points
    feat = jnp.concatenate(
        [
            jnp.zeros((1, rows), F32),
            other_features.transpose(1, 0, 2).reshape(features - 1, rows),
        ],
        axis=0,
    )
    weight_rows = layers * hidden
    chunk_rows = (-(-weight_rows // n) + 15) // 16 * 16
    while weight_rows % chunk_rows:
        chunk_rows += 16
    small_rows = up8(features + layers + 2)
    vm = pltpu.VMEM
    potential, gw, gin, gbias, gout = pl.pallas_call(
        functools.partial(fused_kernel, cap, chunk_rows),
        out_shape=(
            jax.ShapeDtypeStruct(density.shape, density.dtype),
            jax.ShapeDtypeStruct((weight_rows, hidden), F32),
            jax.ShapeDtypeStruct((features, hidden), F32),
            jax.ShapeDtypeStruct((layers + 1, hidden), F32),
            jax.ShapeDtypeStruct((1, hidden), F32),
        ),
        in_specs=[VMEM] * 10,
        out_specs=(VMEM,) * 5,
        scratch_shapes=[
            vm((slots, 2, points, width), BF16),
            vm((slots, 2, points, width), BF16),
            vm((8, slots), jnp.int32),
            vm((n, 8, slots), jnp.int32),
            vm((8, slots), jnp.int32),
            vm((8, slots), jnp.int32),
            pltpu.SMEM((8, slots), jnp.int32),
            vm((batches, n * capp), F32),
            pltpu.SMEM((8, slots), jnp.int32),
            vm((n, capp, 128), F32),
            vm((n, capp, 128), F32),
            vm((rows, hidden), F32),
            vm((batches, 128), F32),
            vm((batches, 128), F32),
            vm((batches, 128), F32),
            vm((small_rows, hidden), F32),
            vm((n * chunk_rows, hidden), F32),
            vm((n, capp + 8, 128), F32),
            vm((n, capp + 8, 128), F32),
            vm((n, chunk_rows, hidden), BF16),
            vm((n, chunk_rows, hidden), BF16),
            vm((chunk_rows, hidden), BF16),
            vm((n, chunk_rows, hidden), BF16),
            vm((8, 128), F32),
            vm((n, 8, 128), F32),
            vm((slots, width, width), F32),
            vm((blocks, width, width), BF16),
            pltpu.SemaphoreType.DMA((7, n)),
            pltpu.SemaphoreType.DMA((7, n)),
            pltpu.SemaphoreType.DMA((2,)),
        ],
        compiler_params=pltpu.CompilerParams(
            vmem_limit_bytes=56 * 1024 * 1024, collective_id=0, has_side_effects=True
        ),
    )(
        block_lists, counts[None, :], ao_values.reshape(total, points, width), density, feat, quad_weights, w_in, biases, w_layers, w_out[None, :],
    )
    return (potential, gw.reshape(layers, hidden, hidden), gin, gbias, gout.reshape(hidden))


def solution(mesh):
    placed = (
        P(("groups", "wide"), None),
        P(("groups", "wide"), None, None, None),
        P(("groups", "wide"), None),
        P(("groups", "wide")),
        P(("groups", "wide"), None, None),
        P(("groups", "wide"), None),
        P(),
        P(),
        P(),
        P(),
    )
    return jax.shard_map(
        shards,
        mesh=mesh,
        in_specs=placed,
        out_specs=(
            P(("groups", "wide"), None),
            P("groups", None, None),
            P("groups", None),
            P("groups", None),
            P("groups"),
        ),
        check_vma=False,
    )
```

```python
import functools

import jax
import jax.numpy as jnp
from jax import lax
from jax.experimental import pallas as pl
from jax.experimental.pallas import tpu as pltpu
from jax.sharding import PartitionSpec as P

highest = lax.Precision.HIGHEST
F32 = jnp.float32
BF16 = jnp.bfloat16
CHUNK = 512
VMEM = pl.BlockSpec(memory_space=pltpu.VMEM)


def up8(x):
    return (x + 7) // 8 * 8


def eye_mask(points):
    return lax.broadcasted_iota(jnp.int32, (points, 128), 0) == lax.broadcasted_iota(
        jnp.int32, (points, 128), 1
    )


def col_dot(a, b):
    return lax.dot_general(a, b, (((0,), (0,)), ((), ())), preferred_element_type=F32)


def fused_kernel(
    cap, rows_each,
    list_ref, count_ref, ao_ref, den_ref, feat_ref, quad_ref,
    win_ref, bias_ref, wl_ref, wout_ref,
    pot_ref, gw_ref, gin_ref, gbias_ref, gout_ref,
    send_ao, recv_ao, pid_msg, recv_pid, table, plan, splan, pick_scr, stable, send_part, ret, pre_scr,
    rho_scr, quad_col_scr, pw_scr, feat_hi, feat_lo, acts_scr, round_scr,
    small, grads, send_w, recv_w, send_m, recv_m, send_g, recv_g, send_a, recv_a, send_s, recv_s,
    prefix, den,
    ssem, rsem, tsem, dsem,
):
    n = send_part.shape[0]
    points, width = ao_ref.shape[1:]
    batches = quad_ref.shape[1]
    rows = points * batches
    hidden = wout_ref.shape[1]
    layers = wl_ref.shape[0]
    features = win_ref.shape[0]
    halves = hidden // 128
    slots = n * cap
    capp = send_part.shape[1]
    blocks = den_ref.shape[1] // width
    me = lax.axis_index("wide")
    eye = eye_mask(points)

    def peer(d):
        return lax.rem(me + d, n)

    def origin(d):
        return lax.rem(me + n - d, n)

    def mine(k):
        return pl.ds(k * cap, cap)

    def copy(phase, src, dst, d):
        return pltpu.make_async_remote_copy(
            src_ref=src, dst_ref=dst, send_sem=ssem.at[phase, d], recv_sem=rsem.at[phase, d],
            device_id={"wide": peer(d)}, device_id_type=pl.DeviceIdType.MESH,
        )

    def each(fn):
        def body(d, carry):
            fn(d)
            return carry

        lax.fori_loop(1, n, body, 0)

    barrier = pltpu.get_barrier_semaphore()

    def greet(d):
        pl.semaphore_signal(
            barrier, inc=1, device_id={"wide": peer(d)}, device_id_type=pl.DeviceIdType.MESH
        )

    each(greet)

    def den_copy(c):
        return pltpu.make_async_copy(
            den_ref.at[:, pl.ds(pl.multiple_of(c * width, width), width)], den.at[c], dsem.at[c]
        )

    def den_start(c, carry):
        den_copy(c).start()
        return carry

    def den_wait(c, carry):
        den_copy(c).wait()
        return carry

    lax.fori_loop(0, blocks, den_start, 0)
    total = batches * 2
    up = lax.broadcasted_iota(jnp.int32, (total, total), 0)
    across = lax.broadcasted_iota(jnp.int32, (total, total), 1)
    square = (batches, batches)
    same = lax.broadcasted_iota(jnp.int32, square, 0) == lax.broadcasted_iota(jnp.int32, square, 1)

    def stand(row):
        return jnp.sum(jnp.where(same, row, 0), axis=1, keepdims=True)

    first_ids = stand(list_ref[0:1, :])
    second_ids = stand(list_ref[1:2, :])
    target = jnp.concatenate([first_ids, second_ids], axis=0)
    partner = jnp.concatenate([second_ids, first_ids], axis=0)
    target_row = jnp.sum(jnp.where(up == across, target, 0), axis=0, keepdims=True)
    earlier = (target_row == target) & (across < up)
    rank = jnp.sum(earlier.astype(jnp.int32), axis=1, keepdims=True)
    used = stand(count_ref[...])
    used = jnp.concatenate([used, used], axis=0)
    entry = lax.broadcasted_iota(jnp.int32, (total, 1), 0)
    second = (entry >= batches).astype(jnp.int32)
    source = 2 * (entry - batches * second) + second
    mate_entry = source + 1 - 2 * second
    slot_no = lax.broadcasted_iota(jnp.int32, (total, slots), 1)
    sits = slot_no == target * cap + rank

    def at_slot(values):
        return jnp.sum(jnp.where(sits, values, 0), axis=0, keepdims=True)

    plan[...] = jnp.zeros_like(plan)
    plan[0:1, :] = at_slot(source)
    plan[1:2, :] = at_slot(mate_entry)
    plan[2:3, :] = at_slot((second < used).astype(jnp.int32))
    plan[3:4, :] = at_slot((1 - second < used).astype(jnp.int32))
    pid_msg[...] = jnp.broadcast_to(at_slot(partner), pid_msg.shape)
    to_plan = pltpu.make_async_copy(plan, splan, tsem.at[1])
    to_plan.start()
    padded = lax.broadcasted_iota(jnp.int32, (batches, n * capp), 1)
    home = target * capp + rank
    pick = (padded == home[0:batches]) | (padded == home[batches:total])
    pick_scr[...] = pick.astype(F32)
    to_plan.wait()

    def fill(k):
        for r in range(cap):
            at = k * cap + r
            e = splan[0, at]
            own = ao_ref[e].astype(F32) * splan[2, at].astype(F32)
            mate = splan[1, at]
            other = ao_ref[mate].astype(F32) * splan[3, at].astype(F32)
            send_ao[k * cap + r, 0] = own.astype(BF16)
            send_ao[k * cap + r, 1] = other.astype(BF16)

    def pid_copy(d):
        return copy(0, pid_msg, recv_pid.at[me], d)

    def pid_back(d):
        return copy(0, pid_msg, recv_pid.at[origin(d)], d)

    def ao_copy(d):
        return copy(1, send_ao.at[mine(peer(d))], recv_ao.at[mine(me)], d)

    def ao_back(d):
        return copy(1, send_ao.at[mine(peer(d))], recv_ao.at[mine(origin(d))], d)

    pl.semaphore_wait(barrier, n - 1)
    each(lambda d: pid_copy(d).start())

    def send_one(d):
        fill(peer(d))
        ao_copy(d).start()

    each(send_one)
    fill(me)
    recv_ao[mine(me)] = send_ao[mine(me)]
    recv_pid[me] = pid_msg[...]

    per = CHUNK // batches
    chunks = rows // CHUNK
    grads[...] = jnp.zeros_like(grads)
    small[...] = jnp.zeros_like(small)
    pw_scr[...] = jnp.zeros_like(pw_scr)
    feat_hi[...] = jnp.zeros_like(feat_hi)
    feat_lo[...] = jnp.zeros_like(feat_lo)
    wide_eye = eye_mask(batches)[:, 0:batches]

    def as_col(block):
        spread = jnp.where(wide_eye[None], block[:, None, :], 0.0)
        return jnp.sum(spread, axis=2, keepdims=True).reshape(CHUNK, 1)

    for k in range(chunks):
        at = k * CHUNK
        block = jnp.concatenate(
            [feat_ref[:, p, :] for p in range(k * per, (k + 1) * per)], axis=1
        )
        part = lax.dot_general(
            block, win_ref[1:features, :], (((0,), (0,)), ((), ())), precision=highest,
            preferred_element_type=F32,
        )
        pre_scr[at : at + CHUNK, :] = part + bias_ref[0:1, :]
        quad_col_scr[at : at + CHUNK, :] = as_col(quad_ref[k * per : (k + 1) * per, :])
        hi = block.astype(BF16)
        feat_hi[0 : features - 1, at : at + CHUNK] = hi
        feat_lo[0 : features - 1, at : at + CHUNK] = (block - hi.astype(F32)).astype(BF16)

    each(lambda d: pid_back(d).wait_recv())
    lists = jnp.max(recv_pid[...], axis=1)
    lane = lax.broadcasted_iota(jnp.int32, (n, slots), 1)
    base = lax.broadcasted_iota(jnp.int32, (n, slots), 0) * cap
    gathered = jnp.zeros((n, slots), jnp.int32)
    for r in range(cap):
        mine_r = jnp.sum(jnp.where(lane == me * cap + r, lists, 0), axis=1, keepdims=True)
        gathered = gathered + jnp.where(lane == base + r, mine_r, 0)
    pid_row = jnp.sum(gathered, axis=0, keepdims=True)
    up = lax.broadcasted_iota(jnp.int32, (slots, slots), 0)
    across = lax.broadcasted_iota(jnp.int32, (slots, slots), 1)
    pid_col = jnp.sum(jnp.where(up == across, pid_row, 0), axis=1, keepdims=True)
    twin = (pid_row == pid_col) & (across < up)
    order = jnp.sum(((pid_row < pid_col) | twin).astype(jnp.int32), axis=1, keepdims=True)
    held = jnp.max(twin.astype(jnp.int32), axis=1, keepdims=True)
    placed = order == across
    table[...] = jnp.zeros_like(table)
    table[0:1, :] = pid_row
    table[1:2, :] = jnp.sum(jnp.where(placed, up, 0), axis=0, keepdims=True)
    table[2:3, :] = jnp.sum(jnp.where(placed, held, 0), axis=0, keepdims=True)
    upto = jnp.sum((pid_col <= across).astype(jnp.int32), axis=0, keepdims=True)
    table[3:4, :] = jnp.maximum(upto - 1, 0)
    table[4:5, :] = jnp.max((pid_col == across).astype(jnp.int32), axis=0, keepdims=True)
    to_scalar = pltpu.make_async_copy(table, stable, tsem.at[0])
    to_scalar.start()
    to_scalar.wait()

    lax.fori_loop(0, blocks, den_wait, 0)
    own = den[me]

    def shares(i):
        rows = []
        for r in range(cap):
            c = stable[0, i * cap + r]
            other = den[c]
            x = recv_ao[i * cap + r, 0]
            y = recv_ao[i * cap + r, 1]
            q = jnp.dot(x, own, preferred_element_type=F32) * x.astype(F32)
            q = q + jnp.dot(x, other, preferred_element_type=F32) * y.astype(F32)
            col = jnp.sum(q, axis=1, keepdims=True)
            rows.append(jnp.sum(jnp.where(eye, col, 0.0), axis=0, keepdims=True))
        if capp > cap:
            rows.append(jnp.zeros((capp - cap, 128), F32))
        return jnp.concatenate(rows, axis=0)

    def part_copy(d):
        return copy(2, send_part.at[peer(d)], ret.at[me], d)

    def part_back(d):
        return copy(2, send_part.at[peer(d)], ret.at[origin(d)], d)

    ret[me] = shares(me)

    def answer(d):
        src = origin(d)
        ao_back(d).wait_recv()
        send_part[src] = shares(src)
        copy(2, send_part.at[src], ret.at[me], n - d).start()

    each(answer)
    each(lambda d: part_back(d).wait_recv())

    rho = lax.dot_general(
        ret[...].reshape(n * capp, 128), pick_scr[...], (((0,), (1,)), ((), ())),
        precision=highest, preferred_element_type=F32,
    )
    rho_scr[...] = rho[0:points, :]
    bias_base = features
    out_row = bias_base + layers + 1
    small_rows = out_row + 1
    holders = hidden // rows_each

    def g_copy(l, d):
        return copy(6 + l, send_g.at[l, lax.rem(peer(d), holders)], recv_g.at[l, me], d)

    def g_back(l, d):
        return copy(6 + l, send_g.at[l, lax.rem(peer(d), holders)], recv_g.at[l, origin(d)], d)

    def a_copy(l, d):
        return copy(6 + layers + l, send_a.at[l], recv_a.at[l, me], d)

    def a_back(l, d):
        return copy(6 + layers + l, send_a.at[l], recv_a.at[l, origin(d)], d)

    def send_grads(l):
        for k in range(holders):
            at = k * rows_each
            send_g[l, k] = grads[l, at : at + rows_each, :].astype(BF16)
        each(lambda d: g_copy(l, d).start())

    def share_grads(l):
        each(lambda d: g_back(l, d).wait_recv())
        recv_g[l, me] = jnp.zeros((rows_each, hidden), BF16)
        at = pl.multiple_of(lax.rem(me, holders) * rows_each, 16)
        added = lax.fori_loop(
            0, n, lambda i, a: a + recv_g[l, i].astype(F32), grads[l, pl.ds(at, rows_each), :]
        )
        send_a[l] = added.astype(BF16)
        each(lambda d: a_copy(l, d).start())
        recv_a[l, me] = added.astype(BF16)

    def step_back(l, row, grad):
        after = acts_scr[l + 1, pl.ds(row, CHUNK), :].astype(F32)
        grad = grad * (1.0 - after * after)
        b = bias_base + l + 1
        small[b : b + 1, :] += jnp.sum(grad, axis=0, keepdims=True)
        return grad.astype(BF16)

    def add_weight(l, row, rounded):
        grads[l] += col_dot(acts_scr[l, pl.ds(row, CHUNK), :], rounded)

    def through(l, rounded):
        return lax.dot_general(
            rounded, wl_ref[l], (((1,), (1,)), ((), ())), preferred_element_type=F32
        )

    def forward(k, carry):
        row = pl.multiple_of(k * CHUNK, CHUNK)
        rho_col = as_col(rho_scr[pl.ds(pl.multiple_of(k * per, per), per), :])
        act = jnp.tanh(pre_scr[pl.ds(row, CHUNK), :] + rho_col * win_ref[0:1, :]).astype(BF16)
        acts_scr[0, pl.ds(row, CHUNK), :] = act
        for l in range(layers):
            inner = jnp.dot(act, wl_ref[l], preferred_element_type=F32)
            act = jnp.tanh(inner + bias_ref[l + 1 : l + 2, :]).astype(BF16)
            acts_scr[l + 1, pl.ds(row, CHUNK), :] = act
        top = act.astype(F32)
        score = jnp.sum(top * wout_ref[...], axis=1, keepdims=True)
        enhance = 2.0 * jax.nn.sigmoid(score)
        weighted = quad_col_scr[pl.ds(row, CHUNK), :] * enhance
        quad_col_scr[pl.ds(row, CHUNK), :] = weighted
        grad_score = weighted * rho_col * (1.0 - 0.5 * enhance)
        small[out_row : out_row + 1, :] += jnp.sum(grad_score * top, axis=0, keepdims=True)
        last = layers - 1
        rounded = step_back(last, row, grad_score * wout_ref[...])
        add_weight(last, row, rounded)
        pre_scr[pl.ds(row, CHUNK), :] = through(last, rounded)
        return carry

    lax.fori_loop(0, chunks, forward, 0)
    send_grads(layers - 1)
    for l in range(layers - 2, 0, -1):

        def middle(k, carry):
            row = pl.multiple_of(k * CHUNK, CHUNK)
            rounded = step_back(l, row, pre_scr[pl.ds(row, CHUNK), :])
            add_weight(l, row, rounded)
            pre_scr[pl.ds(row, CHUNK), :] = through(l, rounded)
            return carry

        lax.fori_loop(0, chunks, middle, 0)
        send_grads(l)

    def bottom(k, carry):
        at = pl.multiple_of(k * per, per)
        row = pl.multiple_of(k * CHUNK, CHUNK)
        rounded = step_back(0, row, pre_scr[pl.ds(row, CHUNK), :])
        round_scr[pl.ds(row, CHUNK), :] = rounded
        grad = through(0, rounded)
        first = acts_scr[0, pl.ds(row, CHUNK), :].astype(F32)
        grad = grad * (1.0 - first * first)
        pre_scr[pl.ds(row, CHUNK), :] = grad
        grad_rho = jnp.sum(grad * win_ref[0:1, :], axis=1, keepdims=True)
        weight = (quad_col_scr[pl.ds(row, CHUNK), :] + grad_rho).reshape(per, batches, 1)
        pw_scr[pl.ds(at, per), 0:batches] = jnp.sum(jnp.where(wide_eye[None], weight, 0.0), axis=1)
        return carry

    lax.fori_loop(0, chunks, bottom, 0)
    send_w[...] = lax.dot_general(
        pick_scr[...], pw_scr[:, 0:batches], (((0,), (1,)), ((), ())), precision=highest,
        preferred_element_type=F32,
    ).reshape(n, capp, 128)

    def w_copy(d):
        return copy(3, send_w.at[peer(d)], recv_w.at[me], d)

    def w_back(d):
        return copy(3, send_w.at[peer(d)], recv_w.at[origin(d)], d)

    def m_copy(d):
        return copy(4, send_m.at[peer(d)], recv_m.at[me], d)

    def m_back(d):
        return copy(4, send_m.at[peer(d)], recv_m.at[origin(d)], d)

    def s_copy(d):
        return copy(5, send_s, recv_s.at[me], d)

    def s_back(d):
        return copy(5, send_s, recv_s.at[origin(d)], d)

    each(lambda d: w_copy(d).start())
    recv_w[me] = send_w[me]

    def late(k, carry):
        row = pl.multiple_of(k * CHUNK, CHUNK)
        add_weight(0, row, round_scr[pl.ds(row, CHUNK), :])
        return carry

    lax.fori_loop(0, chunks, late, 0)
    send_grads(0)

    def late_input(k, carry):
        row = pl.multiple_of(k * CHUNK, CHUNK)
        rho_col = as_col(rho_scr[pl.ds(pl.multiple_of(k * per, per), per), :])
        grad = pre_scr[pl.ds(row, CHUNK), :]
        small[bias_base : bias_base + 1, :] += jnp.sum(grad, axis=0, keepdims=True)
        small[0:1, :] += jnp.sum(grad * rho_col, axis=0, keepdims=True)
        hi = grad.astype(BF16)
        lo = (grad - hi.astype(F32)).astype(BF16)
        fhi = feat_hi[:, pl.ds(row, CHUNK)]
        flo = feat_lo[:, pl.ds(row, CHUNK)]
        term = (
            jnp.dot(fhi, hi, preferred_element_type=F32)
            + jnp.dot(fhi, lo, preferred_element_type=F32)
            + jnp.dot(flo, hi, preferred_element_type=F32)
        )
        small[1:features, :] += term[0 : features - 1]
        return carry

    lax.fori_loop(0, chunks, late_input, 0)
    send_m[...] = jnp.zeros_like(send_m)
    for k in range(small_rows):
        for h in range(halves):
            send_m[k, h : h + 1, :] = small[k : k + 1, h * 128 : (h + 1) * 128]
    each(lambda d: m_copy(d).start())
    recv_m[me] = send_m[me]
    for l in range(layers - 1, 0, -1):
        share_grads(l)
    each(lambda d: w_back(d).wait_recv())

    def own_body(i, acc):
        w = recv_w[i]
        xs, ws = [], []
        for r in range(cap):
            x = recv_ao[i * cap + r, 0]
            col = jnp.sum(jnp.where(eye, w[r : r + 1, :], 0.0), axis=1, keepdims=True)
            weighted = (x.astype(F32) * col).astype(BF16)
            send_ao[i * cap + r, 0] = weighted
            xs.append(x)
            ws.append(weighted)
        return acc + col_dot(jnp.concatenate(ws, axis=0), jnp.concatenate(xs, axis=0))

    each(lambda d: ao_copy(d).wait_send())
    own_sum = lax.fori_loop(0, n, own_body, jnp.zeros((width, width), F32))
    share_grads(0)
    each(lambda d: m_back(d).wait_recv())
    send_s[...] = lax.fori_loop(0, n, lambda i, a: a + recv_m[i], jnp.zeros((8, 128), F32))
    each(lambda d: s_copy(d).start())
    group = 8

    def sorted_body(g, acc):
        for u in range(group):
            j = g * group + u
            s = stable[1, j]
            part = col_dot(send_ao[s, 0], recv_ao[s, 1])
            acc = acc * stable[2, j].astype(F32) + part
            prefix[j] = acc
        return acc

    lax.fori_loop(0, slots // group, sorted_body, jnp.zeros((width, width), F32))

    def out_body(c, carry):
        end = stable[3, c]
        value = prefix[end] * stable[4, c].astype(F32)
        value = value + own_sum * (c == me).astype(F32)
        pot_ref[:, pl.ds(pl.multiple_of(c * width, width), width)] = value.astype(pot_ref.dtype)
        return carry

    lax.fori_loop(0, blocks, out_body, 0)
    recv_s[me] = send_s[...]
    each(lambda d: s_back(d).wait_recv())
    for k in range(small_rows):
        row = jnp.concatenate([recv_s[k, h : h + 1, :] for h in range(halves)], axis=1)
        if k < features:
            gin_ref[k : k + 1, :] = row
        elif k < out_row:
            gbias_ref[k - features : k - features + 1, :] = row
        else:
            gout_ref[...] = row
    for l in range(layers - 1, -1, -1):
        each(lambda d: a_back(l, d).wait_recv())

        def gw_body(k, carry):
            at = pl.multiple_of(k * rows_each, 16)
            gw_ref[l, pl.ds(at, rows_each), :] = recv_a[l, k].astype(F32)
            return carry

        lax.fori_loop(0, holders, gw_body, 0)

    def drain(d):
        pid_copy(d).wait_send()
        part_copy(d).wait_send()
        w_copy(d).wait_send()
        m_copy(d).wait_send()
        s_copy(d).wait_send()
        for l in range(layers):
            g_copy(l, d).wait_send()
            a_copy(l, d).wait_send()

    each(drain)


def shards(
    density, ao_values, block_lists, counts, other_features, quad_weights, w_in, biases, w_layers,
    w_out,
):
    n = lax.axis_size("wide")
    batches, entries, points, width = ao_values.shape
    blocks = density.shape[1] // width
    cap = max(2, (batches * entries + blocks - 1) // blocks)
    capp = up8(cap)
    slots = n * cap
    hidden = w_out.shape[0]
    layers = w_layers.shape[0]
    features = w_in.shape[0]
    total = batches * entries
    rows = batches * points
    rows_each = (-(-hidden // n) + 15) // 16 * 16
    while hidden % rows_each:
        rows_each += 16
    small_rows = up8(features + layers + 2)
    vm = pltpu.VMEM
    potential, gw, gin, gbias, gout = pl.pallas_call(
        functools.partial(fused_kernel, cap, rows_each),
        out_shape=(
            jax.ShapeDtypeStruct(density.shape, density.dtype),
            jax.ShapeDtypeStruct((layers, hidden, hidden), F32),
            jax.ShapeDtypeStruct((features, hidden), F32),
            jax.ShapeDtypeStruct((layers + 1, hidden), F32),
            jax.ShapeDtypeStruct((1, hidden), F32),
        ),
        in_specs=[VMEM] * 3 + [pl.BlockSpec(memory_space=pl.ANY)] + [VMEM] * 6,
        out_specs=(VMEM,) * 5,
        scratch_shapes=[
            vm((slots, 2, points, width), BF16),
            vm((slots, 2, points, width), BF16),
            vm((8, slots), jnp.int32),
            vm((n, 8, slots), jnp.int32),
            vm((8, slots), jnp.int32),
            vm((8, slots), jnp.int32),
            pltpu.SMEM((8, slots), jnp.int32),
            vm((batches, n * capp), F32),
            pltpu.SMEM((8, slots), jnp.int32),
            vm((n, capp, 128), F32),
            vm((n, capp, 128), F32),
            vm((rows, hidden), F32),
            vm((points, batches), F32),
            vm((rows, 1), F32),
            vm((128, 128), F32),
            vm((16, rows), BF16),
            vm((16, rows), BF16),
            vm((layers + 1, rows, hidden), BF16),
            vm((rows, hidden), BF16),
            vm((small_rows, hidden), F32),
            vm((layers, hidden, hidden), F32),
            vm((n, capp, 128), F32),
            vm((n, capp, 128), F32),
            vm((n, 8, 128), F32),
            vm((n, 8, 128), F32),
            vm((layers, hidden // rows_each, rows_each, hidden), BF16),
            vm((layers, n, rows_each, hidden), BF16),
            vm((layers, rows_each, hidden), BF16),
            vm((layers, n, rows_each, hidden), BF16),
            vm((8, 128), F32),
            vm((n, 8, 128), F32),
            vm((slots, width, width), F32),
            vm((blocks, width, width), BF16),
            pltpu.SemaphoreType.DMA((6 + 2 * layers, n)),
            pltpu.SemaphoreType.DMA((6 + 2 * layers, n)),
            pltpu.SemaphoreType.DMA((2,)),
            pltpu.SemaphoreType.DMA((blocks,)),
        ],
        compiler_params=pltpu.CompilerParams(
            vmem_limit_bytes=59 * 1024 * 1024, collective_id=0, has_side_effects=True
        ),
    )(
        block_lists.T, counts[None, :], ao_values.reshape(total, points, width), density, other_features.transpose(1, 2, 0), quad_weights.T, w_in, biases, w_layers, w_out[None, :],
    )
    return (potential, gw, gin, gbias, gout.reshape(hidden))


def solution(mesh):
    placed = (
        P(("groups", "wide"), None),
        P(("groups", "wide"), None, None, None),
        P(("groups", "wide"), None),
        P(("groups", "wide")),
        P(("groups", "wide"), None, None),
        P(("groups", "wide"), None),
        P(),
        P(),
        P(),
        P(),
    )
    return jax.shard_map(
        shards,
        mesh=mesh,
        in_specs=placed,
        out_specs=(
            P(("groups", "wide"), None),
            P("groups", None, None),
            P("groups", None),
            P("groups", None),
            P("groups"),
        ),
        check_vma=False,
    )
```

```python
import functools

import jax
import jax.numpy as jnp
from jax import lax
from jax.experimental import pallas as pl
from jax.experimental.pallas import tpu as pltpu
from jax.sharding import PartitionSpec as P

highest = lax.Precision.HIGHEST
F32 = jnp.float32
BF16 = jnp.bfloat16
CHUNK = 1024
VMEM = pl.BlockSpec(memory_space=pltpu.VMEM)


def up8(x):
    return (x + 7) // 8 * 8


def eye_mask(points):
    return lax.broadcasted_iota(jnp.int32, (points, 128), 0) == lax.broadcasted_iota(
        jnp.int32, (points, 128), 1
    )


def col_dot(a, b):
    return lax.dot_general(a, b, (((0,), (0,)), ((), ())), preferred_element_type=F32)


def fused_kernel(
    cap, rows_each,
    list_ref, count_ref, ao_ref, den_ref, feat_ref, quad_ref,
    win_ref, bias_ref, wl_ref, wout_ref,
    pot_ref, gw_ref, gin_ref, gbias_ref, gout_ref,
    send_ao, recv_ao, pid_msg, recv_pid, table, plan, splan, pick_scr, stable, send_part, ret, pre_scr,
    rho_scr, quad_col_scr, pw_scr, feat_hi, feat_lo, acts_scr, round_scr,
    small, grads, send_w, recv_w, send_m, recv_m, send_g, recv_g, send_a, recv_a, send_s, recv_s,
    prefix, den,
    ssem, rsem, tsem, dsem,
):
    n = send_part.shape[0]
    points, width = ao_ref.shape[1:]
    batches = quad_ref.shape[1]
    rows = points * batches
    hidden = wout_ref.shape[1]
    layers = wl_ref.shape[0]
    features = win_ref.shape[0]
    halves = hidden // 128
    slots = n * cap
    capp = send_part.shape[1]
    blocks = den_ref.shape[1] // width
    me = lax.axis_index("wide")
    eye = eye_mask(points)

    def peer(d):
        return lax.rem(me + d, n)

    def origin(d):
        return lax.rem(me + n - d, n)

    def mine(k):
        return pl.ds(k * cap, cap)

    def copy(phase, src, dst, d):
        return pltpu.make_async_remote_copy(
            src_ref=src, dst_ref=dst, send_sem=ssem.at[phase, d], recv_sem=rsem.at[phase, d],
            device_id={"wide": peer(d)}, device_id_type=pl.DeviceIdType.MESH,
        )

    def each(fn):
        def body(d, carry):
            fn(d)
            return carry

        lax.fori_loop(1, n, body, 0)

    barrier = pltpu.get_barrier_semaphore()

    def greet(d):
        pl.semaphore_signal(
            barrier, inc=1, device_id={"wide": peer(d)}, device_id_type=pl.DeviceIdType.MESH
        )

    each(greet)

    def den_copy(c):
        return pltpu.make_async_copy(
            den_ref.at[:, pl.ds(pl.multiple_of(c * width, width), width)], den.at[c], dsem.at[c]
        )

    def den_start(c, carry):
        den_copy(c).start()
        return carry

    def den_wait(c, carry):
        den_copy(c).wait()
        return carry

    lax.fori_loop(0, blocks, den_start, 0)
    total = batches * 2
    up = lax.broadcasted_iota(jnp.int32, (total, total), 0)
    across = lax.broadcasted_iota(jnp.int32, (total, total), 1)
    square = (batches, batches)
    same = lax.broadcasted_iota(jnp.int32, square, 0) == lax.broadcasted_iota(jnp.int32, square, 1)

    def stand(row):
        return jnp.sum(jnp.where(same, row, 0), axis=1, keepdims=True)

    first_ids = stand(list_ref[0:1, :])
    second_ids = stand(list_ref[1:2, :])
    target = jnp.concatenate([first_ids, second_ids], axis=0)
    partner = jnp.concatenate([second_ids, first_ids], axis=0)
    target_row = jnp.sum(jnp.where(up == across, target, 0), axis=0, keepdims=True)
    earlier = (target_row == target) & (across < up)
    rank = jnp.sum(earlier.astype(jnp.int32), axis=1, keepdims=True)
    used = stand(count_ref[...])
    used = jnp.concatenate([used, used], axis=0)
    entry = lax.broadcasted_iota(jnp.int32, (total, 1), 0)
    second = (entry >= batches).astype(jnp.int32)
    source = 2 * (entry - batches * second) + second
    mate_entry = source + 1 - 2 * second
    slot_no = lax.broadcasted_iota(jnp.int32, (total, slots), 1)
    sits = slot_no == target * cap + rank

    def at_slot(values):
        return jnp.sum(jnp.where(sits, values, 0), axis=0, keepdims=True)

    plan[...] = jnp.zeros_like(plan)
    plan[0:1, :] = at_slot(source)
    plan[1:2, :] = at_slot(mate_entry)
    plan[2:3, :] = at_slot((second < used).astype(jnp.int32))
    plan[3:4, :] = at_slot((1 - second < used).astype(jnp.int32))
    pid_msg[...] = jnp.broadcast_to(at_slot(partner), pid_msg.shape)
    to_plan = pltpu.make_async_copy(plan, splan, tsem.at[1])
    to_plan.start()
    padded = lax.broadcasted_iota(jnp.int32, (batches, n * capp), 1)
    home = target * capp + rank
    pick = (padded == home[0:batches]) | (padded == home[batches:total])
    pick_scr[...] = pick.astype(F32)
    to_plan.wait()

    def fill(k):
        for r in range(cap):
            at = k * cap + r
            e = splan[0, at]
            own = ao_ref[e].astype(F32) * splan[2, at].astype(F32)
            mate = splan[1, at]
            other = ao_ref[mate].astype(F32) * splan[3, at].astype(F32)
            send_ao[k * cap + r, 0] = own.astype(BF16)
            send_ao[k * cap + r, 1] = other.astype(BF16)

    def pid_copy(d):
        return copy(0, pid_msg, recv_pid.at[me], d)

    def pid_back(d):
        return copy(0, pid_msg, recv_pid.at[origin(d)], d)

    def ao_copy(d):
        return copy(1, send_ao.at[mine(peer(d))], recv_ao.at[mine(me)], d)

    def ao_back(d):
        return copy(1, send_ao.at[mine(peer(d))], recv_ao.at[mine(origin(d))], d)

    def fill_body(k, carry):
        fill(k)
        return carry

    lax.fori_loop(0, n, fill_body, 0)
    pl.semaphore_wait(barrier, n - 1)
    each(lambda d: pid_copy(d).start())

    each(lambda d: ao_copy(d).start())
    recv_ao[mine(me)] = send_ao[mine(me)]
    recv_pid[me] = pid_msg[...]

    per = CHUNK // batches
    chunks = rows // CHUNK
    grads[...] = jnp.zeros_like(grads)
    small[...] = jnp.zeros_like(small)
    pw_scr[...] = jnp.zeros_like(pw_scr)
    feat_hi[...] = jnp.zeros_like(feat_hi)
    feat_lo[...] = jnp.zeros_like(feat_lo)
    wide_eye = eye_mask(batches)[:, 0:batches]

    def as_col(block):
        spread = jnp.where(wide_eye[None], block[:, None, :], 0.0)
        return jnp.sum(spread, axis=2, keepdims=True).reshape(CHUNK, 1)

    for k in range(chunks):
        at = k * CHUNK
        block = jnp.concatenate(
            [feat_ref[:, p, :] for p in range(k * per, (k + 1) * per)], axis=1
        )
        part = lax.dot_general(
            block, win_ref[1:features, :], (((0,), (0,)), ((), ())), precision=highest,
            preferred_element_type=F32,
        )
        pre_scr[at : at + CHUNK, :] = part + bias_ref[0:1, :]
        quad_col_scr[at : at + CHUNK, :] = as_col(quad_ref[k * per : (k + 1) * per, :])
        hi = block.astype(BF16)
        feat_hi[0 : features - 1, at : at + CHUNK] = hi
        feat_lo[0 : features - 1, at : at + CHUNK] = (block - hi.astype(F32)).astype(BF16)

    each(lambda d: pid_back(d).wait_recv())
    lists = jnp.max(recv_pid[...], axis=1)
    lane = lax.broadcasted_iota(jnp.int32, (n, slots), 1)
    base = lax.broadcasted_iota(jnp.int32, (n, slots), 0) * cap
    gathered = jnp.zeros((n, slots), jnp.int32)
    for r in range(cap):
        mine_r = jnp.sum(jnp.where(lane == me * cap + r, lists, 0), axis=1, keepdims=True)
        gathered = gathered + jnp.where(lane == base + r, mine_r, 0)
    pid_row = jnp.sum(gathered, axis=0, keepdims=True)
    up = lax.broadcasted_iota(jnp.int32, (slots, slots), 0)
    across = lax.broadcasted_iota(jnp.int32, (slots, slots), 1)
    pid_col = jnp.sum(jnp.where(up == across, pid_row, 0), axis=1, keepdims=True)
    twin = (pid_row == pid_col) & (across < up)
    order = jnp.sum(((pid_row < pid_col) | twin).astype(jnp.int32), axis=1, keepdims=True)
    held = jnp.max(twin.astype(jnp.int32), axis=1, keepdims=True)
    placed = order == across
    table[...] = jnp.zeros_like(table)
    table[0:1, :] = pid_row
    table[1:2, :] = jnp.sum(jnp.where(placed, up, 0), axis=0, keepdims=True)
    table[2:3, :] = jnp.sum(jnp.where(placed, held, 0), axis=0, keepdims=True)
    upto = jnp.sum((pid_col <= across).astype(jnp.int32), axis=0, keepdims=True)
    table[3:4, :] = jnp.maximum(upto - 1, 0)
    table[4:5, :] = jnp.max((pid_col == across).astype(jnp.int32), axis=0, keepdims=True)
    to_scalar = pltpu.make_async_copy(table, stable, tsem.at[0])
    to_scalar.start()
    to_scalar.wait()

    lax.fori_loop(0, blocks, den_wait, 0)
    own = den[me]

    def shares(i):
        rows = []
        for r in range(cap):
            c = stable[0, i * cap + r]
            other = den[c]
            x = recv_ao[i * cap + r, 0]
            y = recv_ao[i * cap + r, 1]
            q = jnp.dot(x, own, preferred_element_type=F32) * x.astype(F32)
            q = q + jnp.dot(x, other, preferred_element_type=F32) * y.astype(F32)
            col = jnp.sum(q, axis=1, keepdims=True)
            rows.append(jnp.sum(jnp.where(eye, col, 0.0), axis=0, keepdims=True))
        if capp > cap:
            rows.append(jnp.zeros((capp - cap, 128), F32))
        return jnp.concatenate(rows, axis=0)

    def part_copy(d):
        return copy(2, send_part.at[peer(d)], ret.at[me], d)

    def part_back(d):
        return copy(2, send_part.at[peer(d)], ret.at[origin(d)], d)

    ret[me] = shares(me)

    def answer(d):
        src = origin(d)
        ao_back(d).wait_recv()
        send_part[src] = shares(src)
        copy(2, send_part.at[src], ret.at[me], n - d).start()

    each(answer)
    each(lambda d: part_back(d).wait_recv())

    rho = lax.dot_general(
        ret[...].reshape(n * capp, 128), pick_scr[...], (((0,), (1,)), ((), ())),
        precision=highest, preferred_element_type=F32,
    )
    rho_scr[...] = rho[0:points, :]
    bias_base = features
    out_row = bias_base + layers + 1
    small_rows = out_row + 1
    holders = hidden // rows_each

    def g_copy(l, d):
        return copy(6 + l, send_g.at[l, lax.rem(peer(d), holders)], recv_g.at[l, me], d)

    def g_back(l, d):
        return copy(6 + l, send_g.at[l, lax.rem(peer(d), holders)], recv_g.at[l, origin(d)], d)

    def a_copy(l, d):
        return copy(6 + layers + l, send_a.at[l], recv_a.at[l, me], d)

    def a_back(l, d):
        return copy(6 + layers + l, send_a.at[l], recv_a.at[l, origin(d)], d)

    def send_grads(l):
        for k in range(holders):
            at = k * rows_each
            send_g[l, k] = grads[l, at : at + rows_each, :].astype(BF16)
        each(lambda d: g_copy(l, d).start())

    def share_grads(l):
        each(lambda d: g_back(l, d).wait_recv())
        recv_g[l, me] = jnp.zeros((rows_each, hidden), BF16)
        at = pl.multiple_of(lax.rem(me, holders) * rows_each, 16)
        added = lax.fori_loop(
            0, n, lambda i, a: a + recv_g[l, i].astype(F32), grads[l, pl.ds(at, rows_each), :]
        )
        send_a[l] = added.astype(BF16)
        each(lambda d: a_copy(l, d).start())
        recv_a[l, me] = added.astype(BF16)

    def step_back(l, row, grad):
        after = acts_scr[l + 1, pl.ds(row, CHUNK), :].astype(F32)
        grad = grad * (1.0 - after * after)
        b = bias_base + l + 1
        small[b : b + 1, :] += jnp.sum(grad, axis=0, keepdims=True)
        return grad.astype(BF16)

    def add_weight(l, row, rounded):
        grads[l] += col_dot(acts_scr[l, pl.ds(row, CHUNK), :], rounded)

    def through(l, rounded):
        return lax.dot_general(
            rounded, wl_ref[l], (((1,), (1,)), ((), ())), preferred_element_type=F32
        )

    def forward(k, carry):
        row = pl.multiple_of(k * CHUNK, CHUNK)
        rho_col = as_col(rho_scr[pl.ds(pl.multiple_of(k * per, per), per), :])
        act = jnp.tanh(pre_scr[pl.ds(row, CHUNK), :] + rho_col * win_ref[0:1, :]).astype(BF16)
        acts_scr[0, pl.ds(row, CHUNK), :] = act
        for l in range(layers):
            inner = jnp.dot(act, wl_ref[l], preferred_element_type=F32)
            act = jnp.tanh(inner + bias_ref[l + 1 : l + 2, :]).astype(BF16)
            acts_scr[l + 1, pl.ds(row, CHUNK), :] = act
        top = act.astype(F32)
        score = jnp.sum(top * wout_ref[...], axis=1, keepdims=True)
        enhance = 2.0 * jax.nn.sigmoid(score)
        weighted = quad_col_scr[pl.ds(row, CHUNK), :] * enhance
        quad_col_scr[pl.ds(row, CHUNK), :] = weighted
        grad_score = weighted * rho_col * (1.0 - 0.5 * enhance)
        small[out_row : out_row + 1, :] += jnp.sum(grad_score * top, axis=0, keepdims=True)
        last = layers - 1
        rounded = step_back(last, row, grad_score * wout_ref[...])
        add_weight(last, row, rounded)
        pre_scr[pl.ds(row, CHUNK), :] = through(last, rounded)
        return carry

    lax.fori_loop(0, chunks, forward, 0)
    send_grads(layers - 1)
    for l in range(layers - 2, 0, -1):

        def middle(k, carry):
            row = pl.multiple_of(k * CHUNK, CHUNK)
            rounded = step_back(l, row, pre_scr[pl.ds(row, CHUNK), :])
            add_weight(l, row, rounded)
            pre_scr[pl.ds(row, CHUNK), :] = through(l, rounded)
            return carry

        lax.fori_loop(0, chunks, middle, 0)
        send_grads(l)

    def bottom(k, carry):
        at = pl.multiple_of(k * per, per)
        row = pl.multiple_of(k * CHUNK, CHUNK)
        rounded = step_back(0, row, pre_scr[pl.ds(row, CHUNK), :])
        round_scr[pl.ds(row, CHUNK), :] = rounded
        grad = through(0, rounded)
        first = acts_scr[0, pl.ds(row, CHUNK), :].astype(F32)
        grad = grad * (1.0 - first * first)
        pre_scr[pl.ds(row, CHUNK), :] = grad
        grad_rho = jnp.sum(grad * win_ref[0:1, :], axis=1, keepdims=True)
        weight = (quad_col_scr[pl.ds(row, CHUNK), :] + grad_rho).reshape(per, batches, 1)
        pw_scr[pl.ds(at, per), 0:batches] = jnp.sum(jnp.where(wide_eye[None], weight, 0.0), axis=1)
        return carry

    lax.fori_loop(0, chunks, bottom, 0)
    send_w[...] = lax.dot_general(
        pick_scr[...], pw_scr[:, 0:batches], (((0,), (1,)), ((), ())), precision=highest,
        preferred_element_type=F32,
    ).reshape(n, capp, 128)

    def w_copy(d):
        return copy(3, send_w.at[peer(d)], recv_w.at[me], d)

    def w_back(d):
        return copy(3, send_w.at[peer(d)], recv_w.at[origin(d)], d)

    def m_copy(d):
        return copy(4, send_m.at[peer(d)], recv_m.at[me], d)

    def m_back(d):
        return copy(4, send_m.at[peer(d)], recv_m.at[origin(d)], d)

    def s_copy(d):
        return copy(5, send_s, recv_s.at[me], d)

    def s_back(d):
        return copy(5, send_s, recv_s.at[origin(d)], d)

    each(lambda d: w_copy(d).start())
    recv_w[me] = send_w[me]

    def late(k, carry):
        row = pl.multiple_of(k * CHUNK, CHUNK)
        add_weight(0, row, round_scr[pl.ds(row, CHUNK), :])
        return carry

    lax.fori_loop(0, chunks, late, 0)
    send_grads(0)

    def late_input(k, carry):
        row = pl.multiple_of(k * CHUNK, CHUNK)
        rho_col = as_col(rho_scr[pl.ds(pl.multiple_of(k * per, per), per), :])
        grad = pre_scr[pl.ds(row, CHUNK), :]
        small[bias_base : bias_base + 1, :] += jnp.sum(grad, axis=0, keepdims=True)
        small[0:1, :] += jnp.sum(grad * rho_col, axis=0, keepdims=True)
        hi = grad.astype(BF16)
        lo = (grad - hi.astype(F32)).astype(BF16)
        fhi = feat_hi[:, pl.ds(row, CHUNK)]
        flo = feat_lo[:, pl.ds(row, CHUNK)]
        term = (
            jnp.dot(fhi, hi, preferred_element_type=F32)
            + jnp.dot(fhi, lo, preferred_element_type=F32)
            + jnp.dot(flo, hi, preferred_element_type=F32)
        )
        small[1:features, :] += term[0 : features - 1]
        return carry

    lax.fori_loop(0, chunks, late_input, 0)
    send_m[...] = jnp.zeros_like(send_m)
    for k in range(small_rows):
        for h in range(halves):
            send_m[k, h : h + 1, :] = small[k : k + 1, h * 128 : (h + 1) * 128]
    each(lambda d: m_copy(d).start())
    recv_m[me] = send_m[me]
    for l in range(layers - 1, 0, -1):
        share_grads(l)
    each(lambda d: w_back(d).wait_recv())

    def own_body(i, acc):
        w = recv_w[i]
        xs, ws = [], []
        for r in range(cap):
            x = recv_ao[i * cap + r, 0]
            col = jnp.sum(jnp.where(eye, w[r : r + 1, :], 0.0), axis=1, keepdims=True)
            weighted = (x.astype(F32) * col).astype(BF16)
            send_ao[i * cap + r, 0] = weighted
            xs.append(x)
            ws.append(weighted)
        return acc + col_dot(jnp.concatenate(ws, axis=0), jnp.concatenate(xs, axis=0))

    each(lambda d: ao_copy(d).wait_send())
    own_sum = lax.fori_loop(0, n, own_body, jnp.zeros((width, width), F32))
    share_grads(0)
    each(lambda d: m_back(d).wait_recv())
    send_s[...] = lax.fori_loop(0, n, lambda i, a: a + recv_m[i], jnp.zeros((8, 128), F32))
    each(lambda d: s_copy(d).start())
    group = 8

    def sorted_body(g, acc):
        for u in range(group):
            j = g * group + u
            s = stable[1, j]
            part = col_dot(send_ao[s, 0], recv_ao[s, 1])
            acc = acc * stable[2, j].astype(F32) + part
            prefix[j] = acc
        return acc

    lax.fori_loop(0, slots // group, sorted_body, jnp.zeros((width, width), F32))

    def out_body(c, carry):
        end = stable[3, c]
        value = prefix[end] * stable[4, c].astype(F32)
        value = value + own_sum * (c == me).astype(F32)
        pot_ref[:, pl.ds(pl.multiple_of(c * width, width), width)] = value.astype(pot_ref.dtype)
        return carry

    lax.fori_loop(0, blocks, out_body, 0)
    recv_s[me] = send_s[...]
    each(lambda d: s_back(d).wait_recv())
    for k in range(small_rows):
        row = jnp.concatenate([recv_s[k, h : h + 1, :] for h in range(halves)], axis=1)
        if k < features:
            gin_ref[k : k + 1, :] = row
        elif k < out_row:
            gbias_ref[k - features : k - features + 1, :] = row
        else:
            gout_ref[...] = row
    for l in range(layers - 1, -1, -1):
        each(lambda d: a_back(l, d).wait_recv())

        def gw_body(k, carry):
            at = pl.multiple_of(k * rows_each, 16)
            gw_ref[l, pl.ds(at, rows_each), :] = recv_a[l, k].astype(F32)
            return carry

        lax.fori_loop(0, holders, gw_body, 0)

    def drain(d):
        pid_copy(d).wait_send()
        part_copy(d).wait_send()
        w_copy(d).wait_send()
        m_copy(d).wait_send()
        s_copy(d).wait_send()
        for l in range(layers):
            g_copy(l, d).wait_send()
            a_copy(l, d).wait_send()

    each(drain)


def shards(
    density, ao_values, block_lists, counts, other_features, quad_weights, w_in, biases, w_layers,
    w_out,
):
    n = lax.axis_size("wide")
    batches, entries, points, width = ao_values.shape
    blocks = density.shape[1] // width
    cap = max(2, (batches * entries + blocks - 1) // blocks)
    capp = up8(cap)
    slots = n * cap
    hidden = w_out.shape[0]
    layers = w_layers.shape[0]
    features = w_in.shape[0]
    total = batches * entries
    rows = batches * points
    rows_each = (-(-hidden // n) + 15) // 16 * 16
    while hidden % rows_each:
        rows_each += 16
    small_rows = up8(features + layers + 2)
    vm = pltpu.VMEM
    potential, gw, gin, gbias, gout = pl.pallas_call(
        functools.partial(fused_kernel, cap, rows_each),
        out_shape=(
            jax.ShapeDtypeStruct(density.shape, density.dtype),
            jax.ShapeDtypeStruct((layers, hidden, hidden), F32),
            jax.ShapeDtypeStruct((features, hidden), F32),
            jax.ShapeDtypeStruct((layers + 1, hidden), F32),
            jax.ShapeDtypeStruct((1, hidden), F32),
        ),
        in_specs=[VMEM] * 3 + [pl.BlockSpec(memory_space=pl.ANY)] + [VMEM] * 6,
        out_specs=(VMEM,) * 5,
        scratch_shapes=[
            vm((slots, 2, points, width), BF16),
            vm((slots, 2, points, width), BF16),
            vm((8, slots), jnp.int32),
            vm((n, 8, slots), jnp.int32),
            vm((8, slots), jnp.int32),
            vm((8, slots), jnp.int32),
            pltpu.SMEM((8, slots), jnp.int32),
            vm((batches, n * capp), F32),
            pltpu.SMEM((8, slots), jnp.int32),
            vm((n, capp, 128), F32),
            vm((n, capp, 128), F32),
            vm((rows, hidden), F32),
            vm((points, batches), F32),
            vm((rows, 1), F32),
            vm((128, 128), F32),
            vm((16, rows), BF16),
            vm((16, rows), BF16),
            vm((layers + 1, rows, hidden), BF16),
            vm((rows, hidden), BF16),
            vm((small_rows, hidden), F32),
            vm((layers, hidden, hidden), F32),
            vm((n, capp, 128), F32),
            vm((n, capp, 128), F32),
            vm((n, 8, 128), F32),
            vm((n, 8, 128), F32),
            vm((layers, hidden // rows_each, rows_each, hidden), BF16),
            vm((layers, n, rows_each, hidden), BF16),
            vm((layers, rows_each, hidden), BF16),
            vm((layers, n, rows_each, hidden), BF16),
            vm((8, 128), F32),
            vm((n, 8, 128), F32),
            vm((slots, width, width), F32),
            vm((blocks, width, width), BF16),
            pltpu.SemaphoreType.DMA((6 + 2 * layers, n)),
            pltpu.SemaphoreType.DMA((6 + 2 * layers, n)),
            pltpu.SemaphoreType.DMA((2,)),
            pltpu.SemaphoreType.DMA((blocks,)),
        ],
        compiler_params=pltpu.CompilerParams(
            vmem_limit_bytes=59 * 1024 * 1024, collective_id=0, has_side_effects=True
        ),
    )(
        block_lists.T, counts[None, :], ao_values.reshape(total, points, width), density, other_features.transpose(1, 2, 0), quad_weights.T, w_in, biases, w_layers, w_out[None, :],
    )
    return (potential, gw, gin, gbias, gout.reshape(hidden))


def solution(mesh):
    placed = (
        P(("groups", "wide"), None),
        P(("groups", "wide"), None, None, None),
        P(("groups", "wide"), None),
        P(("groups", "wide")),
        P(("groups", "wide"), None, None),
        P(("groups", "wide"), None),
        P(),
        P(),
        P(),
        P(),
    )
    return jax.shard_map(
        shards,
        mesh=mesh,
        in_specs=placed,
        out_specs=(
            P(("groups", "wide"), None),
            P("groups", None, None),
            P("groups", None),
            P("groups", None),
            P("groups"),
        ),
        check_vma=False,
    )
```
